256 devices in a mesh: row: 4 (over x), col: 16 (over z, core), rep: 4 (over y).
Axes of the slice: x: 4, y: 4, z: 8, core: 2. Of those that a mesh axis runs over, the one named last changes fastest.
Arguments:
- right_side: float32 [4, 5, 16, 64, 128], P('rep', None, 'row'), may hold values from -6 to 6
- top_right_side: float32 [2, 16, 64, 128], P(None, 'row'), may hold values from -6 to 6
- leaf_upper: bfloat16 [4, 10, 16, 16, 128, 128], P('rep', None, 'col', 'row'), may hold values from -0.125 to 0.125
- leaf_upper_mask: int32 [4, 10, 16, 16], P('rep', None, 'col', 'row'), may hold values from 0 to 1, as said below
- leaf_lower: bfloat16 [4, 10, 16, 16, 128, 128], P('rep', None, 'col', 'row'), may hold values from -0.125 to 0.125
- leaf_lower_mask: int32 [4, 10, 16, 16], P('rep', None, 'col', 'row'), may hold values from 0 to 1, as said below
- cross_upper: bfloat16 [4, 5, 16, 2, 16, 128, 128], P('rep', None, 'col', None, 'row'), may hold values from -0.0625 to 0.0625
- cross_upper_mask: int32 [4, 5, 16, 2, 16], P('rep', None, 'col', None, 'row'), may hold values from 0 to 1, as said below
- cross_lower: bfloat16 [4, 2, 16, 5, 16, 128, 128], P('rep', None, 'col', None, 'row'), may hold values from -0.21875 to 0.21875
- cross_lower_mask: int32 [4, 2, 16, 5, 16], P('rep', None, 'col', None, 'row'), may hold values from 0 to 1, as said below
- top_upper: bfloat16 [1, 16, 16, 128, 128], P(None, 'col', 'row'), may hold values from -0.125 to 0.125
- top_lower: bfloat16 [1, 16, 16, 128, 128], P(None, 'col', 'row'), may hold values from -0.125 to 0.125
- leaf_upper_inverse: float32 [4, 5, 16, 128, 128], P('rep', None, 'row'), as said below
- leaf_lower_inverse: float32 [4, 5, 16, 128, 128], P('rep', None, 'row'), as said below
- top_upper_inverse: float32 [2, 16, 128, 128], P(None, 'row'), as said below
- top_lower_inverse: float32 [2, 16, 128, 128], P(None, 'row'), as said below
- leaf_sizes: int32 [4, 5, 16], P('rep', None, 'row'), may hold values from 32 to 128, as said below
- top_sizes: int32 [2, 16], P(None, 'row'), may hold values from 32 to 128, as said below
Outputs:
- solution: float32 [4, 5, 16, 64, 128], P('rep', None, 'row', 'col')
- top_solution: float32 [2, 16, 64, 128], P(None, 'row', 'col')
The draws below stay inside these ranges and needn't reach their ends.
Inputs may be any that keep to these rules, and one draw needn't show every extreme that they name: `leaf_sizes`: cell counts of the supernodes; the largest and the smallest are each reached in every draw. `top_sizes`: cell counts of the supernodes; the largest and the smallest are each reached in every draw. `leaf_upper_mask`: every supernode has one parent in the next level of the elimination tree (the top leaf level's parents lie in the lowest ancestor level, and ancestors' parents are common to all subtrees); the block pattern is 1 where the later level's supernode is an ancestor of the earlier level's supernode, plus some further fill blocks, else 0; L and U patterns follow the same tree. `leaf_lower_mask`: 1 where the consumed (later level's) supernode is an ancestor of the produced one in the elimination tree, plus some further fill blocks, else 0. `cross_upper_mask`: 1 where the ancestor-level supernode is an ancestor of the leaf supernode in the elimination tree, plus some further fill blocks, else 0. `cross_lower_mask`: 1 where the ancestor-level supernode is an ancestor of the leaf supernode in the elimination tree, plus some further fill blocks, else 0. `leaf_upper_inverse`: each block is the inverse of an upper triangular diagonal block, so it is upper triangular. `leaf_lower_inverse`: each block is the inverse of a unit lower triangular diagonal block, so it is unit lower triangular. `top_upper_inverse`: each block is the inverse of an upper triangular diagonal block, so it is upper triangular. `top_lower_inverse`: each block is the inverse of a unit lower triangular diagonal block, so it is unit lower triangular.
All inputs are finite; a program needn't handle non-finite values.
Results may differ from the reference program's by a relative error of at most 0.014.
Values may be sent and summed in bfloat16 or wider, within the bound.
A program may use at most 64 MiB of HBM per device.

```python
import math
import jax
import jax.numpy as jnp
from jax import lax

S = 128
NRHS = 64
NPL = 16
LEVL = 5
LEVA = 2
LAYERS = 4
PAIRS = 10
PAIRA = 1


def capped_sizes(key, full_shape):
    total_slots = math.prod(full_shape)
    drawn = jax.random.randint(jax.random.fold_in(key, 1), (total_slots,), S // 4, S + 1)
    top_place = jax.random.randint(jax.random.fold_in(key, 2), (), 0, total_slots)
    offset_draw = jax.random.randint(jax.random.fold_in(key, 3), (), 1, total_slots)
    low_place = (top_place + offset_draw) % total_slots
    places = jnp.arange(total_slots)
    drawn = jnp.where(places == top_place, S, drawn)
    drawn = jnp.where(places == low_place, S // 4, drawn)
    return drawn.reshape(full_shape).astype(jnp.int32)


def triangle_inverse(key, leading, lower_side):
    full_shape = leading + (S, S)
    row_index = lax.broadcasted_iota(jnp.int32, full_shape, len(leading))
    col_index = lax.broadcasted_iota(jnp.int32, full_shape, len(leading) + 1)
    scatter_noise = jax.random.normal(jax.random.fold_in(key, 1), full_shape, jnp.float32) * (0.6 / math.sqrt(S))
    if lower_side:
        diagonal = jnp.ones(full_shape, jnp.float32)
        strict = row_index > col_index
    else:
        diagonal = jnp.exp(jax.random.uniform(jax.random.fold_in(key, 2), full_shape, jnp.float32, math.log(0.5), math.log(2.0)))
        strict = row_index < col_index
    return jnp.where(row_index == col_index, diagonal, jnp.where(strict, scatter_noise, 0.0)).astype(jnp.float32)


def tree_ancestors(key):
    leaf_parent = jax.random.randint(jax.random.fold_in(key, 101), (LAYERS, LEVL, NPL), 0, NPL)
    top_parent = jax.random.randint(jax.random.fold_in(key, 102), (LEVA - 1, NPL), 0, NPL)
    level_total = LEVL + LEVA

    def parent_of(level):
        if level < LEVL:
            return leaf_parent[:, level]
        return jnp.broadcast_to(top_parent[level - LEVL][None, :], (LAYERS, NPL))
    table = {}
    for lower_level in range(level_total - 1):
        current = parent_of(lower_level)
        table[lower_level, lower_level + 1] = current
        for higher in range(lower_level + 2, level_total):
            current = jnp.take_along_axis(parent_of(higher - 1), current, axis=1)
            table[lower_level, higher] = current
    return table


def child_rows(ancestor):
    labels = jnp.arange(NPL, dtype=jnp.int32)
    return ancestor[:, :, None] == labels[None, None, :]


def parent_rows(ancestor):
    labels = jnp.arange(NPL, dtype=jnp.int32)
    return ancestor[:, None, :] == labels[None, :, None]


def with_fill(key, pattern):
    extra = jax.random.randint(key, pattern.shape, 0, NPL) < 2
    return jnp.logical_or(pattern, extra).astype(jnp.int32)


def draw_leaf_upper_mask(key, part):
    table = tree_ancestors(key)
    key = jax.random.fold_in(key, 21)
    blocks = []
    for later in range(1, LEVL):
        for earlier in range(later):
            blocks.append(child_rows(table[earlier, later]))
    return with_fill(key, jnp.stack(blocks, axis=1))


def draw_leaf_lower_mask(key, part):
    table = tree_ancestors(key)
    key = jax.random.fold_in(key, 22)
    blocks = []
    for remaining in range(1, LEVL):
        produced = LEVL - 1 - remaining
        for consumed in range(produced + 1, LEVL):
            blocks.append(parent_rows(table[produced, consumed]))
    return with_fill(key, jnp.stack(blocks, axis=1))


def draw_cross_upper_mask(key, part):
    table = tree_ancestors(key)
    key = jax.random.fold_in(key, 23)
    levels = []
    for leaf_level in range(LEVL):
        tops = [child_rows(table[leaf_level, LEVL + top_level]) for top_level in range(LEVA)]
        levels.append(jnp.stack(tops, axis=2))
    return with_fill(key, jnp.stack(levels, axis=1))


def draw_cross_lower_mask(key, part):
    table = tree_ancestors(key)
    key = jax.random.fold_in(key, 24)
    tops = []
    for top_level in range(LEVA):
        leaves = [parent_rows(table[leaf_level, LEVL + top_level]) for leaf_level in range(LEVL)]
        tops.append(jnp.stack(leaves, axis=2))
    return with_fill(key, jnp.stack(tops, axis=1))


def draw_leaf_upper_inverse(key, part):
    key = jax.random.fold_in(key, 11)
    return triangle_inverse(key, (LAYERS, LEVL, NPL), False)


def draw_leaf_lower_inverse(key, part):
    key = jax.random.fold_in(key, 12)
    return triangle_inverse(key, (LAYERS, LEVL, NPL), True)


def draw_top_upper_inverse(key, part):
    key = jax.random.fold_in(key, 13)
    return triangle_inverse(key, (LEVA, NPL), False)


def draw_top_lower_inverse(key, part):
    key = jax.random.fold_in(key, 14)
    return triangle_inverse(key, (LEVA, NPL), True)


def draw_leaf_sizes(key, part):
    key = jax.random.fold_in(key, 15)
    return capped_sizes(key, (LAYERS, LEVL, NPL))


def draw_top_sizes(key, part):
    key = jax.random.fold_in(key, 16)
    return capped_sizes(key, (LEVA, NPL))


def shard_levels(own_key, dims, shards, smallest, largest):
    loudness = 1.0
    for axis_at, parts in shards:
        heights = jax.random.uniform(jax.random.fold_in(jax.random.fold_in(own_key, 6), axis_at), (parts,), jnp.float32, smallest / len(shards), largest / len(shards))
        loudness = loudness * jnp.repeat(jnp.exp(heights), dims[axis_at] // parts).reshape((-1,) + (1,) * (len(dims) - 1 - axis_at))
    return loudness


def scatter_about(own_key, dims, spread, bound, cuts=(), kind=jnp.bfloat16):
    values = jax.random.normal(own_key, dims, jnp.float32) * spread
    if len(cuts) > 0:
        values = shard_levels(own_key, dims, cuts, -0.22, 0.18) * values
    return jnp.clip(values, min=-bound, max=bound).astype(kind)


def setup_inputs(seed: int = 0) -> dict:
    splits = jax.random.split(jax.random.key(seed), 19)
    right_side = scatter_about(splits[0], (LAYERS, LEVL, NPL, NRHS, S), 1.0, 6.0, ((0, 4), (2, 4)), jnp.float32)
    top_right_side = scatter_about(splits[1], (LEVA, NPL, NRHS, S), 1.0, 6.0, ((1, 4),), jnp.float32)
    leaf_upper = scatter_about(splits[2], (LAYERS, PAIRS, NPL, NPL, S, S), (S * LEVL * 3) ** -0.5, 0.125, ((0, 4), (2, 16), (3, 4)))
    leaf_upper_mask = draw_leaf_upper_mask(jax.random.fold_in(splits[18], 71), 0)
    leaf_lower = scatter_about(splits[4], (LAYERS, PAIRS, NPL, NPL, S, S), (S * LEVL * 3) ** -0.5, 0.125, ((0, 4), (2, 16), (3, 4)))
    leaf_lower_mask = draw_leaf_lower_mask(jax.random.fold_in(splits[18], 71), 0)
    cross_upper = scatter_about(splits[6], (LAYERS, LEVL, NPL, LEVA, NPL, S, S), (LAYERS * LEVL * S * 3) ** -0.5, 0.0625, ((0, 4), (2, 16), (4, 4)))
    cross_upper_mask = draw_cross_upper_mask(jax.random.fold_in(splits[18], 71), 0)
    cross_lower = scatter_about(splits[8], (LAYERS, LEVA, NPL, LEVL, NPL, S, S), (LEVA * S * 3) ** -0.5, 0.21875, ((0, 4), (2, 16), (4, 4)))
    cross_lower_mask = draw_cross_lower_mask(jax.random.fold_in(splits[18], 71), 0)
    top_upper = scatter_about(splits[10], (PAIRA, NPL, NPL, S, S), (NPL * S) ** -0.5, 0.125, ((1, 16), (2, 4)))
    top_lower = scatter_about(splits[11], (PAIRA, NPL, NPL, S, S), (NPL * S) ** -0.5, 0.125, ((1, 16), (2, 4)))
    leaf_upper_inverse = draw_leaf_upper_inverse(jax.random.fold_in(splits[18], 71), 0)
    leaf_lower_inverse = draw_leaf_lower_inverse(jax.random.fold_in(splits[18], 71), 0)
    top_upper_inverse = draw_top_upper_inverse(jax.random.fold_in(splits[18], 71), 0)
    top_lower_inverse = draw_top_lower_inverse(jax.random.fold_in(splits[18], 71), 0)
    leaf_sizes = draw_leaf_sizes(jax.random.fold_in(splits[18], 71), 0)
    top_sizes = draw_top_sizes(jax.random.fold_in(splits[18], 71), 0)
    return dict(right_side=right_side, top_right_side=top_right_side, leaf_upper=leaf_upper, leaf_upper_mask=leaf_upper_mask, leaf_lower=leaf_lower, leaf_lower_mask=leaf_lower_mask, cross_upper=cross_upper, cross_upper_mask=cross_upper_mask, cross_lower=cross_lower, cross_lower_mask=cross_lower_mask, top_upper=top_upper, top_lower=top_lower, leaf_upper_inverse=leaf_upper_inverse, leaf_lower_inverse=leaf_lower_inverse, top_upper_inverse=top_upper_inverse, top_lower_inverse=top_lower_inverse, leaf_sizes=leaf_sizes, top_sizes=top_sizes)


def live_cells(size_table, cell_count):
    positions = lax.broadcasted_iota(jnp.int32, size_table.shape + (cell_count,), size_table.ndim)
    return (positions < size_table[..., None]).astype(jnp.float32)


def block_terms(vectors, blocks, pattern):
    source = blocks.astype(jnp.float32)
    if pattern is not None:
        source = source * pattern.astype(jnp.float32)[..., None, None]
    return jnp.einsum("qjrs,qjkst->krt", vectors.astype(jnp.float32), source)


def apply_inverse(residue, inverse, live_mask):
    masked = residue * live_mask[:, None, :]
    solved = jnp.einsum("krs,kst->krt", masked, inverse, precision=lax.Precision.HIGHEST)
    return solved * live_mask[:, None, :]


def reference(right_side, top_right_side, leaf_upper, leaf_upper_mask, leaf_lower, leaf_lower_mask, cross_upper, cross_upper_mask, cross_lower, cross_lower_mask, top_upper, top_lower, leaf_upper_inverse, leaf_lower_inverse, top_upper_inverse, top_lower_inverse, leaf_sizes, top_sizes):
    leaf_live = live_cells(leaf_sizes, S)
    top_live = live_cells(top_sizes, S)
    forward = []
    crossing = jnp.zeros((LEVA, NPL, NRHS, S), jnp.float32)
    for subtree in range(LAYERS):
        solved_tiers = []
        rounded_tiers = []
        for tier_index in range(LEVL):
            residue = right_side[subtree, tier_index]
            if tier_index > 0:
                first_pair = tier_index * (tier_index - 1) // 2
                earlier = jnp.stack(rounded_tiers)
                residue = residue - block_terms(earlier, leaf_upper[subtree, first_pair:first_pair + tier_index], leaf_upper_mask[subtree, first_pair:first_pair + tier_index])
            solved = apply_inverse(residue, leaf_upper_inverse[subtree, tier_index], leaf_live[subtree, tier_index])
            solved_tiers.append(solved)
            rounded_tiers.append(solved.astype(jnp.bfloat16))
        forward.append(solved_tiers)
        stacked = jnp.stack(rounded_tiers).astype(jnp.float32)
        masked = cross_upper[subtree].astype(jnp.float32) * cross_upper_mask[subtree].astype(jnp.float32)[..., None, None]
        crossing = crossing + jnp.einsum("mjrs,mjakst->akrt", stacked, masked)
    top_forward = []
    top_rounded = []
    for tier_index in range(LEVA):
        coupled = crossing[tier_index]
        if tier_index > 0:
            first_pair = tier_index * (tier_index - 1) // 2
            coupled = coupled + block_terms(jnp.stack(top_rounded), top_upper[first_pair:first_pair + tier_index], None)
        solved = apply_inverse(top_right_side[tier_index] - coupled, top_upper_inverse[tier_index], top_live[tier_index])
        top_forward.append(solved)
        top_rounded.append(solved.astype(jnp.bfloat16))
    top_final = [None] * LEVA
    top_back = [None] * LEVA
    for step_index in range(LEVA):
        tier_index = LEVA - 1 - step_index
        residue = top_forward[tier_index]
        if step_index > 0:
            first_pair = step_index * (step_index - 1) // 2
            later_cols = jnp.stack([top_back[m] for m in range(tier_index + 1, LEVA)])
            residue = residue - block_terms(later_cols, top_lower[first_pair:first_pair + step_index], None)
        solved = apply_inverse(residue, top_lower_inverse[tier_index], top_live[tier_index])
        top_final[tier_index] = solved
        top_back[tier_index] = solved.astype(jnp.bfloat16)
    top_stack = jnp.stack(top_back).astype(jnp.float32)
    solution = []
    for subtree in range(LAYERS):
        masked = cross_lower[subtree].astype(jnp.float32) * cross_lower_mask[subtree].astype(jnp.float32)[..., None, None]
        from_top = jnp.einsum("ajrs,ajlkst->lkrt", top_stack, masked)
        leaf_final = [None] * LEVL
        leaf_back = [None] * LEVL
        for step_index in range(LEVL):
            tier_index = LEVL - 1 - step_index
            coupled = from_top[tier_index]
            if step_index > 0:
                first_pair = step_index * (step_index - 1) // 2
                later_cols = jnp.stack([leaf_back[m] for m in range(tier_index + 1, LEVL)])
                coupled = coupled + block_terms(later_cols, leaf_lower[subtree, first_pair:first_pair + step_index], leaf_lower_mask[subtree, first_pair:first_pair + step_index])
            solved = apply_inverse(forward[subtree][tier_index] - coupled, leaf_lower_inverse[subtree, tier_index], leaf_live[subtree, tier_index])
            leaf_final[tier_index] = solved
            leaf_back[tier_index] = solved.astype(jnp.bfloat16)
        solution.append(jnp.stack(leaf_final))
    return jnp.stack(solution), jnp.stack(top_final)
```

```python
import jax
import jax.numpy as jnp
from jax import lax
from jax.experimental import pallas as pl
from jax.experimental.pallas import tpu as pltpu
from jax.sharding import PartitionSpec as P

MESH = pl.DeviceIdType.MESH
BF = jnp.bfloat16
F32 = jnp.float32

LU, CU, CL, LL, TU, TL = 0, 10, 20, 30, 40, 41
LUI, LLI, TUI, TLI = 0, 5, 10, 12


def upper_pair(m, l):
    return LU + l * (l - 1) // 2 + m


def lower_pair(l, m):
    q = 4 - l
    return LL + q * (q - 1) // 2 + (m - l - 1)


def kernel(
    rs, trs, lu, ll, cu, cl, tu, tl, lui, lli, tui, tli,
    lum, llm, cum, clm, ls, ts,
    sol, top,
    blk, inv_raw, inv, rhs, trhs, acc, y_keep,
    s_leaf, r_leaf, s_cross, r_cross, s_top1, r_top1, s_top0, r_top0, xt1,
    s_last, r_last, s_out, r_out,
    load_sem, pair_ssem, pair_rsem, leaf_ssem, leaf_rsem, top_ssem, top_rsem, out_ssem, out_rsem,
):
    x = lax.axis_index("row")
    c = lax.axis_index("col")
    r = lax.axis_index("rep")
    z, h = c // 2, lax.rem(c, 2)
    sibling = {"col": c + 1 - 2 * h}
    is_owner = (z // 2) == x
    low = jnp.where(z == 2 * x, 1.0, 0.0).astype(F32)
    high = jnp.where(z == 2 * x + 1, 1.0, 0.0).astype(F32)

    half = pl.ds(pl.multiple_of(32 * h, 32), 32)
    loads = {}

    def load(name, src, dst):
        copy = pltpu.make_async_copy(src, dst, load_sem.at[len(loads)])
        copy.start()
        loads[name] = copy

    load("lui0", lui.at[0, pl.ds(0, 1)], inv_raw.at[pl.ds(LUI, 1)])
    load("rhs", rs.at[0, :, :, half], rhs)
    load("lu", lu.at[0, :, 0], blk.at[pl.ds(LU, 10), h])
    load("lui", lui.at[0, pl.ds(1, 4)], inv_raw.at[pl.ds(LUI + 1, 4)])
    for m in range(5):
        load(("cu", m), cu.at[0, m, 0], blk.at[pl.ds(CU + 2 * m, 2), h])
    load("trhs", trs.at[:, :, half], trhs)
    load("tui", tui, inv_raw.at[pl.ds(TUI, 2)])
    load("tli", tli, inv_raw.at[pl.ds(TLI, 2)])
    load("tu", tu.at[0], blk.at[pl.ds(TU, 1), h])
    load("tl", tl.at[0], blk.at[pl.ds(TL, 1), h])
    for a in range(2):
        load(("cl", a), cl.at[0, a, 0], blk.at[pl.ds(CL + 5 * a, 5), h])
    load("lli", lli.at[0], inv_raw.at[pl.ds(LLI, 5)])
    load("ll", ll.at[0, :, 0], blk.at[pl.ds(LL, 10), h])

    barrier = pltpu.get_barrier_semaphore()

    def greet(device, is_self=None):
        if is_self is None:
            pl.semaphore_signal(barrier, inc=1, device_id=device, device_id_type=MESH)
        else:
            @pl.when(jnp.logical_not(is_self))
            def _():
                pl.semaphore_signal(barrier, inc=1, device_id=device, device_id_type=MESH)

    greet(sibling)
    for e in range(1, 4):
        greet({"rep": lax.rem(r + e, 4)})
    for d in range(8):
        zz = lax.rem(z + d, 8)
        greet({"col": 2 * zz + c // 8}, (h == c // 8) if d == 0 else None)
        for e in range(4):
            greet(
                {"row": z // 2, "col": 2 * zz + h, "rep": lax.rem(r + e, 4)},
                is_owner if d == 0 and e == 0 else None,
            )

    def barrier_wait():
        others = 42 + jnp.where(is_owner, 0, 1) + jnp.where(h == c // 8, 0, 1)
        pl.semaphore_wait(barrier, others)

    def split(value):
        hi = value.astype(BF)
        return hi, (value - hi.astype(F32)).astype(BF)

    def masked_inverse(place, k, size):
        value = inv_raw[place, k]
        row = lax.broadcasted_iota(jnp.int32, (128, 128), 0)
        col = lax.broadcasted_iota(jnp.int32, (128, 128), 1)
        return jnp.where(jnp.maximum(row, col) < size, value, 0.0)

    def keep_inverse(place, k, value):
        hi, lo = split(value)
        inv[place, k, :, 0:128] = hi
        inv[place, k, :, 128:256] = lo

    def prepare_inverses(first, count, size_of):
        for i in range(count):
            for k in range(4):
                keep_inverse(first + i, k, masked_inverse(first + i, k, size_of(i, k)))

    def times_inverse(value, place, k):
        rows = value.shape[0]
        hi, lo = split(value)
        both = jnp.concatenate([hi, lo], axis=0)
        out = jnp.dot(both, inv[place, k], preferred_element_type=F32)
        return out[:rows, :128] + out[rows:, :128] + out[:rows, 128:]

    def apply_inverses(value, place):
        return [times_inverse(value[:, 128 * k : 128 * (k + 1)], place, k) for k in range(4)]

    def contract(vectors, pair):
        columns = [
            jnp.concatenate([blk[pair, 0, k], blk[pair, 1, k]], axis=0) for k in range(4)
        ]
        return jnp.dot(vectors, jnp.concatenate(columns, axis=1), preferred_element_type=F32)

    def mask_blocks(first, count, flag_of):
        def body(i, _):
            for k in range(4):
                flag = jnp.full((128, 128), flag_of(i, k).astype(F32), F32).astype(BF)
                blk[first + i, h, k] = blk[first + i, h, k] * flag
            return 0

        lax.fori_loop(0, count, body, 0)

    shared = {}

    def share(name, first, count):
        at = len(shared)
        part = blk.at[pl.ds(first, count), h]
        copy = pltpu.make_async_remote_copy(
            src_ref=part, dst_ref=part, send_sem=pair_ssem.at[at], recv_sem=pair_rsem.at[at],
            device_id=sibling, device_id_type=MESH,
        )
        copy.start()
        shared[name] = copy

    def rows_of(source, level_rows, scale):
        return jnp.concatenate([source[level_rows, k] * scale for k in range(4)], axis=1)

    def owned(value):
        return jnp.concatenate([value * low, value * high], axis=1)

    def copy_out(src, dst, ssem, rsem, device, is_self=None):
        remote = pltpu.make_async_remote_copy(
            src_ref=src, dst_ref=dst, send_sem=ssem, recv_sem=rsem, device_id=device, device_id_type=MESH
        )
        if is_self is None:
            remote.start()
            return

        @pl.when(is_self)
        def _():
            pltpu.make_async_copy(src, dst, rsem).start()

        @pl.when(jnp.logical_not(is_self))
        def _():
            remote.start()

    def await_bytes(ref, sem):
        pltpu.make_async_copy(ref, ref, sem).wait()

    def leaf_send(step, parts):
        for q in range(2):
            for i in range(2):
                s_leaf[step, q, i] = parts[2 * q + i].astype(BF)
        for d in (2, 1, 3, 0):
            for q in range(2):
                copy_out(
                    s_leaf.at[step, q], r_leaf.at[step, z], leaf_ssem.at[step], leaf_rsem.at[step],
                    {"row": lax.rem(x + d, 4), "col": 4 * x + 2 * q + h},
                    (z == 2 * x + q) if d == 0 else None,
                )

    def leaf_sent(step):
        await_bytes(r_leaf.at[step, pl.ds(0, 7)], leaf_ssem.at[step])

        @pl.when(jnp.logical_not(is_owner))
        def _():
            await_bytes(r_leaf.at[step, 7], leaf_ssem.at[step])

    def leaf_receive(step):
        await_bytes(r_leaf.at[step], leaf_rsem.at[step])
        both = []
        for i in range(2):
            total = r_leaf[step, 0, i].astype(F32)
            for zz in range(1, 8):
                total = total + r_leaf[step, zz, i].astype(F32)
            both.append(total)
        return jnp.concatenate(both, axis=1)

    def pack(parts, rows, q):
        return jnp.concatenate([parts[2 * q][rows], parts[2 * q + 1][rows]], axis=0)

    def wide_send(source_of, dst, at):
        for e in (2, 1, 3, 0):
            for d in (2, 1, 3, 0):
                for q in range(2):
                    rr = lax.rem(r + e, 4)
                    copy_out(
                        source_of(q, rr), dst.at[r, z], top_ssem.at[at], top_rsem.at[at],
                        {"row": lax.rem(x + d, 4), "col": 4 * x + 2 * q + h, "rep": rr},
                        (z == 2 * x + q) if d == 0 and e == 0 else None,
                    )

    def wide_sent(dst, at):
        await_bytes(dst.at[pl.ds(0, 3)], top_ssem.at[at])
        await_bytes(dst.at[3, pl.ds(0, 7)], top_ssem.at[at])

        @pl.when(jnp.logical_not(is_owner))
        def _():
            await_bytes(dst.at[3, 7], top_ssem.at[at])

    def out_send(place, value):
        for i in range(4):
            for k in range(2):
                s_out[place, i, k] = value[8 * i : 8 * (i + 1), 128 * k : 128 * (k + 1)]

        @pl.when(is_owner)
        def _():
            for d in range(8):
                n = lax.rem(lax.rem(c, 8) + d, 8)
                copy_out(
                    s_out.at[place, n // 2], r_out.at[place, lax.rem(z, 2)],
                    out_ssem.at[place], out_rsem.at[0],
                    {"col": 8 * h + n}, (c // 8 == h) if d == 0 else None,
                )

    def out_sent(place):
        @pl.when(is_owner)
        def _():
            await_bytes(s_out.at[place], out_ssem.at[place])
            await_bytes(s_out.at[place, pl.ds(0, 3)], out_ssem.at[place])

            @pl.when(c // 8 != h)
            def _():
                await_bytes(s_out.at[place, 3], out_ssem.at[place])

    loads["lui0"].wait()
    prepare_inverses(LUI, 1, lambda i, k: ls[0, i, k])
    loads["rhs"].wait()
    first_parts = apply_inverses(rows_of(rhs, 0, 0.125), LUI)
    for l in range(1, 5):
        acc[l] = rows_of(rhs, l, 0.125)
    loads["lu"].wait()
    mask_blocks(LU, 10, lambda i, k: lum[0, i, 0, k])
    loads["lui"].wait()
    prepare_inverses(LUI + 1, 4, lambda i, k: ls[0, i + 1, k])
    barrier_wait()

    leaf_send(0, first_parts)
    for l in range(1, 5):
        share(("lu", l), upper_pair(0, l), l)
    for m in range(5):
        loads["cu", m].wait()
        mask_blocks(CU + 2 * m, 2, lambda i, k, m=m: cum[0, m, 0, i, k])
        share(("cu", m), CU + 2 * m, 2)
    loads["tu"].wait()
    loads["tl"].wait()
    share("top", TU, 2)
    loads["trhs"].wait()
    for a in range(2):
        acc[5 + a] = rows_of(trhs, a, 0.03125)
    leaf_sent(0)
    shared["lu", 1].wait_recv()
    y = leaf_receive(0)
    y_keep[0] = y

    for l in range(1, 5):
        yb = y.astype(BF)
        residue = acc[l] - contract(yb, upper_pair(l - 1, l))
        leaf_send(l, apply_inverses(residue, LUI + l))
        if l == 1:
            for a in range(2):
                loads["cl", a].wait()
                mask_blocks(CL + 5 * a, 5, lambda i, k, a=a: clm[0, a, 0, i, k])
                share(("cl", a), CL + 5 * a, 5)
        if l == 2:
            loads["ll"].wait()
            mask_blocks(LL, 10, lambda i, k: llm[0, i, 0, k])
            share("ll", LL, 10)
        if l == 3:
            loads["tui"].wait()
            loads["tli"].wait()
            prepare_inverses(TUI, 1, lambda i, k: ts[i, k])
            prepare_inverses(TLI, 2, lambda i, k: ts[i, k])
            for k in range(4):
                upper = masked_inverse(TUI + 1, k, ts[1, k])
                keep_inverse(TUI + 1, k, times_inverse(upper, TLI + 1, k))
        if l == 4:
            loads["lli"].wait()
            prepare_inverses(LLI, 5, lambda i, k: ls[0, i, k])
        for later in range(l + 1, 5):
            if l == 1:
                shared["lu", later].wait_recv()
            acc[later] = acc[later] - contract(yb, upper_pair(l - 1, later))
        shared["cu", l - 1].wait_recv()
        for a in range(2):
            acc[5 + a] = acc[5 + a] - contract(yb, CU + 2 * (l - 1) + a)
        leaf_sent(l)
        y = leaf_receive(l)
        y_keep[l] = y

    yb = y.astype(BF)
    shared["cu", 4].wait_recv()
    for a in range(2):
        residue = acc[5 + a] - contract(yb, CU + 8 + a)
        parts = apply_inverses(residue, TUI + a)
        for q in range(2):
            for rr in range(4):
                s_cross[a, q, rr] = pack(parts, slice(8 * rr, 8 * rr + 8), q).astype(BF)
        wide_send(lambda q, rr, a=a: s_cross.at[a, q, rr], r_cross.at[a], a)
    shared["top"].wait_recv()
    for a in range(2):
        wide_sent(r_cross.at[a], a)

    def wide_total(ref):
        total = ref[0].astype(F32)
        for i in range(1, ref.shape[0]):
            total = total + ref[i].astype(F32)
        return total

    def side_by_side(value):
        return jnp.concatenate([value[:8], value[8:]], axis=1)

    await_bytes(r_cross.at[0], top_rsem.at[0])
    top0 = side_by_side(sum(wide_total(r_cross.at[0, rr]) for rr in range(4)))

    parts = apply_inverses(-contract(top0.astype(BF), TU), TUI + 1)
    everyone = slice(0, 8)
    for q in range(2):
        s_top1[q] = pack(parts, everyone, q).astype(BF)
    for d in (2, 1, 3, 0):
        for q in range(2):
            copy_out(
                s_top1.at[q], r_top1.at[z], top_ssem.at[2], top_rsem.at[2],
                {"row": lax.rem(x + d, 4), "col": 4 * x + 2 * q + h},
                (z == 2 * x + q) if d == 0 else None,
            )
    await_bytes(r_cross.at[1], top_rsem.at[1])
    early = sum(wide_total(r_cross.at[1, rr]) for rr in range(4))
    await_bytes(r_top1.at[pl.ds(0, 7)], top_ssem.at[2])

    @pl.when(jnp.logical_not(is_owner))
    def _():
        await_bytes(r_top1.at[7], top_ssem.at[2])

    await_bytes(r_top1, top_rsem.at[2])
    mine = early + wide_total(r_top1)

    residue = owned(top0) - contract(side_by_side(mine).astype(BF), TL)
    parts = apply_inverses(residue, TLI)
    for q in range(2):
        s_top0[q] = pack(parts, everyone, q).astype(BF)
    wide_send(lambda q, rr: s_top0.at[q], r_top0, 3)
    xt1[r] = mine
    for e in range(1, 4):
        copy_out(
            xt1.at[r], xt1.at[r], top_ssem.at[4], top_rsem.at[4], {"rep": lax.rem(r + e, 4)}
        )
    for l in range(5):
        acc[l] = owned(y_keep[l])
    await_bytes(xt1.at[pl.ds(0, 3)], top_ssem.at[4])
    await_bytes(xt1.at[pl.ds(0, 3)], top_rsem.at[4])

    def from_reps(quarters):
        return jnp.concatenate(
            [jnp.concatenate([q[8 * k : 8 * k + 8] for q in quarters], axis=0) for k in range(2)], axis=1
        )

    x_top1 = from_reps([xt1[rr] for rr in range(4)])
    out_send(5, x_top1)
    xb = x_top1.astype(BF)
    shared["cl", 1].wait_recv()
    for l in range(4, -1, -1):
        acc[l] = acc[l] - contract(xb, CL + 5 + l)
    shared["cl", 0].wait_recv()
    shared["ll"].wait_recv()
    wide_sent(r_top0, 3)
    await_bytes(r_top0, top_rsem.at[3])
    solved = from_reps([wide_total(r_top0.at[rr]) for rr in range(4)])

    for l in range(4, -1, -1):
        xb = solved.astype(BF)
        if l == 4:
            pair_of = lambda low_level: CL + low_level
        else:
            pair_of = lambda low_level, l=l: lower_pair(low_level, l + 1)
        residue = acc[l] - contract(xb, pair_of(l))
        parts = apply_inverses(residue, LLI + l)
        if l > 0:
            step = 9 - l
            leaf_send(step, parts)
        else:
            for i in range(4):
                for q in range(2):
                    s_last[i, q] = pack(parts, slice(8 * i, 8 * i + 8), q).astype(BF)
            for d in (4, 3, 5, 2, 6, 1, 7, 0):
                n = lax.rem(lax.rem(c, 8) + d, 8)
                copy_out(
                    s_last.at[n // 2], r_last.at[z], top_ssem.at[5], top_rsem.at[5],
                    {"col": 8 * h + n}, (c // 8 == h) if d == 0 else None,
                )
        out_send(4 if l == 4 else l, solved)
        for earlier in range(l - 1, -1, -1):
            acc[earlier] = acc[earlier] - contract(xb, pair_of(earlier))
        if l > 0:
            leaf_sent(step)
            solved = leaf_receive(step)

    for copy in shared.values():
        copy.wait_send()
    for place in range(6):
        out_sent(place)
    await_bytes(r_last.at[pl.ds(0, 7)], top_ssem.at[5])

    @pl.when(h != c // 8)
    def _():
        await_bytes(r_last.at[7], top_ssem.at[5])

    def own_rows(value):
        return jnp.where(h == 0, value[0:4], value[4:8])

    await_bytes(r_out, out_rsem.at[0])
    for place in range(6):
        for k in range(4):
            value = own_rows(r_out[place, k // 2, k % 2])
            if place == 5:
                top[1, k] = value
            elif place == 4:
                top[0, k] = value
            else:
                sol[0, place + 1, k] = value
    await_bytes(r_last, top_rsem.at[5])
    last = wide_total(r_last)
    for k in range(4):
        sol[0, 0, k] = own_rows(last[k // 2, 8 * (k % 2) : 8 * (k % 2) + 8])


def on_device(
    right_side, top_right_side, leaf_upper, leaf_upper_mask, leaf_lower, leaf_lower_mask, cross_upper, cross_upper_mask,
    cross_lower, cross_lower_mask, top_upper, top_lower, leaf_upper_inverse, leaf_lower_inverse, top_upper_inverse,
    top_lower_inverse, leaf_sizes, top_sizes,
):
    in_hbm = pl.BlockSpec(memory_space=pl.ANY)
    in_smem = pl.BlockSpec(memory_space=pltpu.SMEM)
    in_vmem = pl.BlockSpec(memory_space=pltpu.VMEM)
    dma = pltpu.SemaphoreType.DMA
    return pl.pallas_call(
        kernel,
        out_shape=(
            jax.ShapeDtypeStruct((1, 5, 4, 4, 128), F32),
            jax.ShapeDtypeStruct((2, 4, 4, 128), F32),
        ),
        in_specs=[in_hbm] * 12 + [in_smem] * 6,
        out_specs=(in_vmem, in_vmem),
        scratch_shapes=[
            pltpu.VMEM((42, 2, 4, 128, 128), BF),
            pltpu.VMEM((14, 4, 128, 128), F32),
            pltpu.VMEM((14, 4, 128, 256), BF),
            pltpu.VMEM((5, 4, 32, 128), F32),
            pltpu.VMEM((2, 4, 32, 128), F32),
            pltpu.VMEM((7, 32, 512), F32),
            pltpu.VMEM((5, 32, 256), F32),
            pltpu.VMEM((9, 2, 2, 32, 128), BF),
            pltpu.VMEM((9, 8, 2, 32, 128), BF),
            pltpu.VMEM((2, 2, 4, 16, 128), BF),
            pltpu.VMEM((2, 4, 8, 16, 128), BF),
            pltpu.VMEM((2, 16, 128), BF),
            pltpu.VMEM((8, 16, 128), BF),
            pltpu.VMEM((2, 16, 128), BF),
            pltpu.VMEM((4, 8, 16, 128), BF),
            pltpu.VMEM((4, 16, 128), F32),
            pltpu.VMEM((4, 2, 16, 128), BF),
            pltpu.VMEM((8, 2, 16, 128), BF),
            pltpu.VMEM((6, 4, 2, 8, 128), F32),
            pltpu.VMEM((6, 2, 2, 8, 128), F32),
            dma((18,)),
            dma((13,)),
            dma((13,)),
            dma((9,)),
            dma((9,)),
            dma((6,)),
            dma((6,)),
            dma((6,)),
            dma((1,)),
        ],
        compiler_params=pltpu.CompilerParams(
            collective_id=0, has_side_effects=True, vmem_limit_bytes=58 * 1024 * 1024
        ),
    )(
        right_side, top_right_side, leaf_upper, leaf_lower, cross_upper, cross_lower, top_upper, top_lower,
        leaf_upper_inverse, leaf_lower_inverse, top_upper_inverse, top_lower_inverse,
        leaf_upper_mask, leaf_lower_mask, cross_upper_mask, cross_lower_mask, leaf_sizes, top_sizes,
    )


def solution(mesh):
    in_specs = (
        P("rep", None, "row", None, None),
        P(None, "row", None, None),
        P("rep", None, "col", "row", None, None),
        P("rep", None, "col", "row"),
        P("rep", None, "col", "row", None, None),
        P("rep", None, "col", "row"),
        P("rep", None, "col", None, "row", None, None),
        P("rep", None, "col", None, "row"),
        P("rep", None, "col", None, "row", None, None),
        P("rep", None, "col", None, "row"),
        P(None, "col", "row", None, None),
        P(None, "col", "row", None, None),
        P("rep", None, "row", None, None),
        P("rep", None, "row", None, None),
        P(None, "row", None, None),
        P(None, "row", None, None),
        P("rep", None, "row"),
        P(None, "row"),
    )
    out_specs = (P("rep", None, "row", "col", None), P(None, "row", "col", None))
    return jax.shard_map(
        on_device, mesh=mesh, in_specs=in_specs, out_specs=out_specs, check_vma=False
    )
```

```python
import jax
import jax.numpy as jnp
from jax import lax
from jax.experimental import pallas as pl
from jax.experimental.pallas import tpu as pltpu
from jax.sharding import PartitionSpec as P

MESH = pl.DeviceIdType.MESH
BF = jnp.bfloat16
F32 = jnp.float32

LU, CU, CL, LL, TU, TL = 0, 10, 20, 30, 40, 41
LUI, LLI, TUI, TLI = 0, 5, 10, 12


def upper_pair(m, l):
    return LU + l * (l - 1) // 2 + m


def lower_pair(l, m):
    q = 4 - l
    return LL + q * (q - 1) // 2 + (m - l - 1)


TURNED = (
    (upper_pair(1, 2), LUI + 2),
    (upper_pair(3, 4), LUI + 4),
    (TL, TLI),
    (lower_pair(3, 4), LLI + 3),
    (lower_pair(1, 2), LLI + 1),
)


def kernel(
    rs, trs, lu, ll, cu, cl, tu, tl, lui, lli, tui, tli,
    lum, llm, cum, clm, ls, ts,
    sol, top,
    blk, inv_raw, inv, rhs, trhs, acc, y_keep, base,
    turn_out, turn,
    s_z, r_z, s_x, r_x, s_zr, r_zr, r_d,
    s_cross, r_cross, s_top0, r_top0, s_mid, r_mid, s_low, r_low, xt0, xt1,
    s_last, r_last, s_out, r_out,
    load_sem, pair_ssem, pair_rsem, z_ssem, z_rsem, x_ssem, x_rsem, zr_ssem, zr_rsem, d_ssem, d_rsem,
    t_ssem, t_rsem, ts_ssem, ts_rsem, top_ssem, top_rsem, out_ssem, out_rsem,
):
    x = lax.axis_index("row")
    c = lax.axis_index("col")
    r = lax.axis_index("rep")
    z, h = c // 2, lax.rem(c, 2)
    even = lax.rem(z, 2) == 0
    first_k = 2 * lax.rem(z, 2)
    sibling = {"col": c + 1 - 2 * h}
    is_owner = (z // 2) == x
    owner = jnp.where(is_owner, 1.0, 0.0).astype(F32)
    low = jnp.where(z == 2 * x, 1.0, 0.0).astype(F32)
    high = jnp.where(z == 2 * x + 1, 1.0, 0.0).astype(F32)

    def row(d):
        return lax.rem(x + d, 4)

    def chip(d):
        return 2 * lax.rem(z + d, 8) + h

    half = pl.ds(pl.multiple_of(32 * h, 32), 32)
    loads = {}

    def load(name, src, dst):
        copy = pltpu.make_async_copy(src, dst, load_sem.at[len(loads)])
        copy.start()
        loads[name] = copy

    load("lui0", lui.at[0, pl.ds(0, 1)], inv_raw.at[pl.ds(LUI, 1)])
    load("rhs", rs.at[0, :, :, half], rhs)
    load("lu", lu.at[0, :, 0], blk.at[pl.ds(LU, 10), h])
    load("lui", lui.at[0, pl.ds(1, 4)], inv_raw.at[pl.ds(LUI + 1, 4)])
    for m in range(5):
        load(("cu", m), cu.at[0, m, 0], blk.at[pl.ds(CU + 2 * m, 2), h])
    load("trhs", trs.at[:, :, half], trhs)
    load("tui", tui, inv_raw.at[pl.ds(TUI, 2)])
    load("tli", tli, inv_raw.at[pl.ds(TLI, 2)])
    load("tu", tu.at[0], blk.at[pl.ds(TU, 1), h])
    load("tl", tl.at[0], blk.at[pl.ds(TL, 1), h])
    for a in range(2):
        load(("cl", a), cl.at[0, a, 0], blk.at[pl.ds(CL + 5 * a, 5), h])
    load("lli", lli.at[0], inv_raw.at[pl.ds(LLI, 5)])
    load("ll", ll.at[0, :, 0], blk.at[pl.ds(LL, 10), h])

    barrier = pltpu.get_barrier_semaphore()

    def greet(device, is_self=None):
        if is_self is None:
            pl.semaphore_signal(barrier, inc=1, device_id=device, device_id_type=MESH)
        else:
            @pl.when(jnp.logical_not(is_self))
            def _():
                pl.semaphore_signal(barrier, inc=1, device_id=device, device_id_type=MESH)

    for d in (4, 3, 5, 2, 6, 1, 7, 0):
        zz = lax.rem(z + d, 8)
        greet({"row": z // 2, "col": 2 * zz + h}, is_owner if d == 0 else None)
        greet({"col": 2 * zz + c // 8}, (h == c // 8) if d == 0 else None)
        if d:
            greet({"col": 2 * zz + h})
    for e in range(4):
        for d in range(4):
            if d or e:
                greet({"row": row(d), "rep": lax.rem(r + e, 4)})
    greet(sibling)

    def barrier_wait():
        others = 37 + jnp.where(is_owner, 0, 1) + jnp.where(h == c // 8, 0, 1)
        pl.semaphore_wait(barrier, others)

    def split(value):
        hi = value.astype(BF)
        return hi, (value - hi.astype(F32)).astype(BF)

    def masked_inverse(place, k, size):
        value = inv_raw[place, k]
        down = lax.broadcasted_iota(jnp.int32, (128, 128), 0)
        across = lax.broadcasted_iota(jnp.int32, (128, 128), 1)
        return jnp.where(jnp.maximum(down, across) < size, value, 0.0)

    def keep_inverse(place, k, value):
        hi, lo = split(value)
        inv[place, k, :, 0:128] = hi
        inv[place, k, :, 128:256] = lo

    def prepare_inverses(first, count, size_of):
        for i in range(count):
            for k in range(4):
                keep_inverse(first + i, k, masked_inverse(first + i, k, size_of(i, k)))

    def times_inverse(value, place, k):
        rows = value.shape[0]
        hi, lo = split(value)
        both = jnp.concatenate([hi, lo], axis=0)
        out = jnp.dot(both, inv[place, k], preferred_element_type=F32)
        return out[:rows, :128] + out[rows:, :128] + out[:rows, 128:]

    def cut(value):
        return [value[:, 128 * k : 128 * (k + 1)] for k in range(value.shape[1] // 128)]

    def apply_inverses(value, place):
        return [times_inverse(part, place, k) for k, part in enumerate(cut(value))]

    def own_pair_inverse(pair, place):
        return jnp.concatenate(
            [times_inverse(part, place, first_k + i) for i, part in enumerate(cut(pair))], axis=1
        )

    def contract(vectors, pair):
        columns = [
            jnp.concatenate([blk[pair, 0, k], blk[pair, 1, k]], axis=0) for k in range(4)
        ]
        return jnp.dot(vectors, jnp.concatenate(columns, axis=1), preferred_element_type=F32)

    def contract_turned(vectors, u):
        columns = [
            jnp.concatenate([turn[u, j, i] for j in range(4)], axis=0) for i in range(2)
        ]
        return jnp.dot(vectors, jnp.concatenate(columns, axis=1), preferred_element_type=F32)

    def mask_blocks(first, count, flag_of):
        def body(i, _):
            for k in range(4):
                flag = jnp.full((128, 128), flag_of(i, k).astype(F32), F32).astype(BF)
                blk[first + i, h, k] = blk[first + i, h, k] * flag
            return 0

        lax.fori_loop(0, count, body, 0)

    def remote_copy(src, dst, ssem, rsem, device):
        return pltpu.make_async_remote_copy(
            src_ref=src, dst_ref=dst, send_sem=ssem, recv_sem=rsem, device_id=device, device_id_type=MESH
        )

    def copy_out(src, dst, ssem, rsem, device, is_self=None):
        remote = remote_copy(src, dst, ssem, rsem, device)
        if is_self is None:
            remote.start()
            return

        @pl.when(is_self)
        def _():
            pltpu.make_async_copy(src, dst, rsem).start()

        @pl.when(jnp.logical_not(is_self))
        def _():
            remote.start()

    def await_bytes(ref, sem):
        pltpu.make_async_copy(ref, ref, sem).wait()

    shared = {}

    def share(name, first, count):
        at = len(shared)
        part = blk.at[pl.ds(first, count), h]
        copy = remote_copy(part, part, pair_ssem.at[at], pair_rsem.at[at], sibling)
        copy.start()
        shared[name] = copy

    def rows_of(source, level, scale):
        return jnp.concatenate([source[level, k] * scale for k in range(4)], axis=1)

    def owned(pair):
        return jnp.concatenate([pair * low, pair * high], axis=1)

    def own_pair(value):
        return jnp.where(even, value[:, :256], value[:, 256:])

    def turn_send(u):
        pair, place = TURNED[u]
        for k in range(4):
            out = jnp.dot(blk[pair, h, k], inv[place, k], preferred_element_type=F32)
            turn_out[u, k // 2, k % 2] = (out[:, :128] + out[:, 128:]).astype(BF)
        for q in range(2):
            copy_out(
                turn_out.at[u, q], turn.at[u, lax.rem(c, 4)], t_ssem.at[u], t_rsem.at[u],
                {"row": c // 4, "col": 4 * x + 2 * q + h}, z == 2 * x + q,
            )

    def turn_share(u):
        await_bytes(turn.at[u, pl.ds(0, 2)], t_rsem.at[u])
        await_bytes(turn_out.at[u, 0], t_ssem.at[u])

        @pl.when(jnp.logical_not(is_owner))
        def _():
            await_bytes(turn_out.at[u, 1], t_ssem.at[u])

        for j in range(2):
            part = turn.at[u, 2 * j + h]
            remote_copy(part, part, ts_ssem.at[u], ts_rsem.at[u], sibling).start()

    def turn_ready(u):
        await_bytes(turn.at[u, pl.ds(0, 2)], ts_ssem.at[u])
        await_bytes(turn.at[u, pl.ds(0, 2)], ts_rsem.at[u])

    def z_send(step, parts):
        for k in range(4):
            s_z[step, k] = parts[k].astype(BF)
        for d in (4, 3, 5, 2, 6, 1, 7):
            copy_out(s_z.at[step], r_z.at[step, z], z_ssem.at[step], z_rsem.at[step], {"col": chip(d)})

    def z_receive(step, parts):
        await_bytes(r_z.at[step, pl.ds(0, 7)], z_ssem.at[step])
        await_bytes(r_z.at[step, pl.ds(0, 7)], z_rsem.at[step])
        totals = []
        for k in range(4):
            total = parts[k]
            for d in range(1, 8):
                total = total + r_z[step, lax.rem(z + d, 8), k].astype(F32)
            totals.append(total)
        return jnp.concatenate(totals, axis=1)

    def x_send(step, pair):
        for i, part in enumerate(cut(pair)):
            s_x[step, i] = part.astype(BF)
        for d in (2, 1, 3):
            copy_out(s_x.at[step], r_x.at[step, x], x_ssem.at[step], x_rsem.at[step], {"row": row(d)})

    def x_receive(step, pair):
        await_bytes(r_x.at[step, pl.ds(0, 3)], x_ssem.at[step])
        await_bytes(r_x.at[step, pl.ds(0, 3)], x_rsem.at[step])
        totals = []
        for i, total in enumerate(cut(pair)):
            for d in range(1, 4):
                total = total + r_x[step, row(d), i].astype(F32)
            totals.append(total)
        return jnp.concatenate(totals, axis=1)

    def gather_send(u, parts):
        for k in range(4):
            s_zr[u, k // 2, k % 2] = parts[k].astype(BF)
        for q in range(2):
            @pl.when(z != 2 * x + q)
            def _(q=q):
                copy_out(
                    s_zr.at[u, q], r_zr.at[u, z], zr_ssem.at[u], zr_rsem.at[u], {"col": 4 * x + 2 * q + h}
                )
        base[...] = own_pair(jnp.concatenate(parts, axis=1))

    def gather_receive(u):
        await_bytes(s_zr.at[u, 0], zr_ssem.at[u])

        @pl.when(jnp.logical_not(is_owner))
        def _():
            await_bytes(s_zr.at[u, 1], zr_ssem.at[u])
            base[...] = jnp.zeros_like(base)

        @pl.when(is_owner)
        def _():
            await_bytes(r_zr.at[u, pl.ds(0, 7)], zr_rsem.at[u])
            for i in range(2):
                total = base[:, 128 * i : 128 * (i + 1)]
                for d in range(1, 8):
                    total = total + r_zr[u, lax.rem(z + d, 8), i].astype(F32)
                base[:, 128 * i : 128 * (i + 1)] = total

    def spread_send(u, pair):
        @pl.when(is_owner)
        def _():
            for i, part in enumerate(cut(pair)):
                r_d[u, i] = part.astype(BF)
            for d in (2, 1, 3):
                copy_out(r_d.at[u], r_d.at[u], d_ssem.at[u], d_rsem.at[u], {"row": row(d)})

    def spread_receive(u):
        @pl.when(is_owner)
        def _():
            for d in range(3):
                await_bytes(r_d.at[u], d_ssem.at[u])

        @pl.when(jnp.logical_not(is_owner))
        def _():
            await_bytes(r_d.at[u], d_rsem.at[u])

        return jnp.concatenate([r_d[u, 0], r_d[u, 1]], axis=1)

    def pack(parts, rows):
        return [jnp.concatenate([parts[2 * q][rows], parts[2 * q + 1][rows]], axis=0) for q in range(2)]

    def unpack(value):
        return jnp.concatenate([value[:8], value[8:]], axis=1)

    def from_reps(ref):
        return jnp.concatenate(
            [jnp.concatenate([ref[rr, 8 * k : 8 * k + 8] for rr in range(4)], axis=0) for k in range(2)],
            axis=1,
        )

    def out_send(place, value):
        for i in range(4):
            for k in range(2):
                s_out[place, i, k] = value[8 * i : 8 * (i + 1), 128 * k : 128 * (k + 1)]

        @pl.when(is_owner)
        def _():
            for d in range(8):
                n = lax.rem(lax.rem(c, 8) + d, 8)
                copy_out(
                    s_out.at[place, n // 2], r_out.at[place, lax.rem(z, 2)],
                    out_ssem.at[place], out_rsem.at[0],
                    {"col": 8 * h + n}, (c // 8 == h) if d == 0 else None,
                )

    def out_sent(place):
        @pl.when(is_owner)
        def _():
            await_bytes(s_out.at[place], out_ssem.at[place])
            await_bytes(s_out.at[place, pl.ds(0, 3)], out_ssem.at[place])

            @pl.when(c // 8 != h)
            def _():
                await_bytes(s_out.at[place, 3], out_ssem.at[place])

    def subtract(level, vectors, pair):
        acc[level] = acc[level] - contract(vectors, pair)

    loads["lui0"].wait()
    prepare_inverses(LUI, 1, lambda i, k: ls[k, i])
    loads["rhs"].wait()
    y0 = own_pair_inverse(jnp.concatenate([rhs[0, first_k], rhs[0, first_k + 1]], axis=1), LUI)
    y_keep[0] = y0
    for l in range(1, 5):
        acc[l] = rows_of(rhs, l, 0.125)
    loads["lu"].wait()
    mask_blocks(LU, 10, lambda i, k: lum[k, i])
    loads["lui"].wait()
    prepare_inverses(LUI + 1, 4, lambda i, k: ls[k, i + 1])
    barrier_wait()

    spread_send(0, y0)
    for l in range(1, 5):
        share(("lu", l), upper_pair(0, l), l)
    turn_send(0)
    for m in range(5):
        loads["cu", m].wait()
        mask_blocks(CU + 2 * m, 2, lambda i, k, m=m: cum[i, k, m])
    share("cu", CU, 10)
    loads["trhs"].wait()
    for a in range(2):
        acc[5 + a] = rows_of(trhs, a, 0.03125)
    shared["lu", 1].wait_recv()
    y0b = spread_receive(0)

    parts = apply_inverses(acc[1] - contract(y0b, upper_pair(0, 1)), LUI + 1)
    z_send(0, parts)
    shared["lu", 2].wait_recv()
    gather_send(0, apply_inverses(acc[2] - contract(y0b, upper_pair(0, 2)), LUI + 2))
    shared["lu", 3].wait_recv()
    shared["lu", 4].wait_recv()
    for l in (3, 4):
        subtract(l, y0b, upper_pair(0, l))
    shared["cu"].wait_recv()
    for a in range(2):
        subtract(5 + a, y0b, CU + a)
    turn_share(0)
    gather_receive(0)
    turn_ready(0)
    y1 = z_receive(0, parts)

    pair = base[...] - contract_turned(y1.astype(BF), 0)
    x_send(0, pair)
    own = own_pair(y1)
    y_keep[1] = own
    spread_send(1, own)
    turn_send(1)
    y1b = spread_receive(1)
    subtract(3, y1b, upper_pair(1, 3))
    y2 = x_receive(0, pair)
    y_keep[2] = y2
    y2b = y2.astype(BF)

    parts = apply_inverses(acc[3] - contract(y2b, upper_pair(2, 3)), LUI + 3)
    z_send(1, parts)
    gather_send(
        1,
        apply_inverses(
            acc[4] - contract(y1b, upper_pair(1, 4)) - contract(y2b, upper_pair(2, 4)), LUI + 4
        ),
    )
    for a in range(2):
        acc[5 + a] = acc[5 + a] - contract(y1b, CU + 2 + a) - contract(y2b, CU + 4 + a)
    loads["tui"].wait()
    loads["tli"].wait()
    prepare_inverses(TUI, 1, lambda i, k: ts[i, k])
    prepare_inverses(TLI, 2, lambda i, k: ts[i, k])
    for k in range(4):
        upper = masked_inverse(TUI + 1, k, ts[1, k])
        keep_inverse(TUI + 1, k, times_inverse(upper, TLI + 1, k))
    turn_share(1)
    gather_receive(1)
    turn_ready(1)
    y3 = z_receive(1, parts)

    pair = base[...] - contract_turned(y3.astype(BF), 1)
    x_send(1, pair)
    own = own_pair(y3)
    y_keep[3] = own
    spread_send(2, own)
    loads["tu"].wait()
    loads["tl"].wait()
    turn_send(2)
    share("top", TU, 1)
    y3b = spread_receive(2)
    for a in range(2):
        subtract(5 + a, y3b, CU + 6 + a)
    y4 = x_receive(1, pair)
    y_keep[4] = y4
    y4b = y4.astype(BF)

    crossing = []
    for a in range(2):
        parts = apply_inverses(acc[5 + a] - contract(y4b, CU + 8 + a), TUI + a)
        for rr in range(4):
            for q, packed in enumerate(pack(parts, slice(8 * rr, 8 * rr + 8))):
                s_cross[a, rr, q] = packed
        for e in (2, 1, 3):
            rr = lax.rem(r + e, 4)
            copy_out(
                s_cross.at[a, rr], r_cross.at[a, r], top_ssem.at[a], top_rsem.at[a], {"rep": rr}
            )
    for a in range(2):
        loads["cl", a].wait()
        mask_blocks(CL + 5 * a, 5, lambda i, k, a=a: clm[a, k, i])
    share("cl", CL, 10)

    def cross_receive(a):
        await_bytes(r_cross.at[a, pl.ds(0, 3)], top_ssem.at[a])
        await_bytes(r_cross.at[a, pl.ds(0, 3)], top_rsem.at[a])
        totals = []
        for q in range(2):
            total = s_cross[a, r, q]
            for e in range(1, 4):
                total = total + r_cross[a, lax.rem(r + e, 4), q]
            totals.append(total)
        return totals

    for q, packed in enumerate(cross_receive(0)):
        s_top0[q] = packed.astype(BF)
    for d in (2, 1, 3, 0):
        for q in range(2):
            copy_out(
                s_top0.at[q], r_top0.at[z], top_ssem.at[2], top_rsem.at[2],
                {"row": row(d), "col": 4 * x + 2 * q + h},
                (z == 2 * x + q) if d == 0 else None,
            )
    crossing = cross_receive(1)
    loads["lli"].wait()
    prepare_inverses(LLI, 5, lambda i, k: ls[k, i])
    loads["ll"].wait()
    mask_blocks(LL, 10, lambda i, k: llm[k, i])
    share("ll", LL, 10)
    turn_share(2)
    turn_ready(2)
    shared["top"].wait_recv()
    await_bytes(r_top0.at[pl.ds(0, 7)], top_ssem.at[2])

    @pl.when(jnp.logical_not(is_owner))
    def _():
        await_bytes(r_top0.at[7], top_ssem.at[2])

    await_bytes(r_top0, top_rsem.at[2])
    top0 = r_top0[0].astype(F32)
    for zz in range(1, 8):
        top0 = top0 + r_top0[zz].astype(F32)
    top0 = unpack(top0)

    parts = [-part for part in apply_inverses(contract(top0.astype(BF), TU), TUI + 1)]
    mine = [crossing[q] + packed for q, packed in enumerate(pack(parts, slice(0, 8)))]
    for q in range(2):
        s_mid[q] = mine[q].astype(BF)
    for d in (4, 3, 5, 2, 6, 1, 7):
        copy_out(s_mid, r_mid.at[z], top_ssem.at[3], top_rsem.at[3], {"col": chip(d)})
    turn_send(3)
    top0_base = own_pair_inverse(top0, TLI) * owner
    await_bytes(r_mid.at[pl.ds(0, 7)], top_ssem.at[3])
    await_bytes(r_mid.at[pl.ds(0, 7)], top_rsem.at[3])
    for q in range(2):
        for d in range(1, 8):
            mine[q] = mine[q] + r_mid[lax.rem(z + d, 8), q].astype(F32)

    vectors = jnp.concatenate([unpack(mine[q]) for q in range(2)], axis=1).astype(BF)
    pair = top0_base - contract_turned(vectors, 2)
    quarter = jnp.concatenate(cut(pair), axis=0)
    s_low[...] = quarter.astype(BF)
    for d in (2, 1, 3):
        copy_out(s_low, r_low.at[x], top_ssem.at[4], top_rsem.at[4], {"row": row(d)})

    @pl.when(is_owner)
    def _():
        xt1[r] = jnp.where(even, mine[0], mine[1])
        for e in (2, 1, 3, 0):
            for d in (2, 1, 3, 0):
                if d or e:
                    copy_out(
                        xt1.at[r], xt1.at[r], top_ssem.at[6], top_rsem.at[6],
                        {"row": row(d), "rep": lax.rem(r + e, 4)},
                    )

    for l in range(5):
        acc[l] = owned(y_keep[l])
    await_bytes(r_low.at[pl.ds(0, 3)], top_ssem.at[4])
    await_bytes(r_low.at[pl.ds(0, 3)], top_rsem.at[4])
    for d in range(1, 4):
        quarter = quarter + r_low[row(d)].astype(F32)
    xt0[r] = quarter
    for e in (2, 1, 3):
        copy_out(
            xt0.at[r], xt0.at[r], top_ssem.at[5], top_rsem.at[5], {"rep": lax.rem(r + e, 4)}
        )
    turn_send(4)

    @pl.when(is_owner)
    def _():
        for _ in range(5):
            await_bytes(xt1.at[pl.ds(0, 3)], top_ssem.at[6])
        await_bytes(xt1.at[pl.ds(0, 3)], top_rsem.at[6])

    @pl.when(jnp.logical_not(is_owner))
    def _():
        await_bytes(xt1, top_rsem.at[6])

    x_top1 = from_reps(xt1)
    xt1b = x_top1.astype(BF)
    shared["cl"].wait_recv()
    subtract(4, xt1b, CL + 9)
    await_bytes(xt0.at[pl.ds(0, 3)], top_ssem.at[5])
    await_bytes(xt0.at[pl.ds(0, 3)], top_rsem.at[5])
    x_top0 = from_reps(xt0)
    xt0b = x_top0.astype(BF)

    parts = apply_inverses(acc[4] - contract(xt0b, CL + 4), LLI + 4)
    z_send(2, parts)
    gather_send(
        2, apply_inverses(acc[3] - contract(xt1b, CL + 8) - contract(xt0b, CL + 3), LLI + 3)
    )
    out_send(5, x_top1)
    out_send(4, x_top0)
    for l in (2, 1, 0):
        acc[l] = acc[l] - contract(xt1b, CL + 5 + l) - contract(xt0b, CL + l)
    turn_share(3)
    gather_receive(2)
    turn_ready(3)
    x4 = z_receive(2, parts)

    pair = base[...] - contract_turned(x4.astype(BF), 3)
    x_send(2, pair)
    own = own_pair(x4)
    spread_send(3, own)
    out_send(3, own)
    shared["ll"].wait_recv()
    x4b = spread_receive(3)
    subtract(2, x4b, lower_pair(2, 4))
    x3 = x_receive(2, pair)
    x3b = x3.astype(BF)

    parts = apply_inverses(acc[2] - contract(x3b, lower_pair(2, 3)), LLI + 2)
    z_send(3, parts)
    gather_send(
        3,
        apply_inverses(
            acc[1] - contract(x4b, lower_pair(1, 4)) - contract(x3b, lower_pair(1, 3)), LLI + 1
        ),
    )
    out_send(2, x3)
    acc[0] = acc[0] - contract(x4b, lower_pair(0, 4)) - contract(x3b, lower_pair(0, 3))
    turn_share(4)
    gather_receive(3)
    turn_ready(4)
    x2 = z_receive(3, parts)

    pair = base[...] - contract_turned(x2.astype(BF), 4)
    x_send(3, pair)
    own = own_pair(x2)
    spread_send(4, own)
    out_send(1, own)
    x2b = spread_receive(4)
    subtract(0, x2b, lower_pair(0, 2))
    x1 = x_receive(3, pair)
    x1b = x1.astype(BF)

    parts = apply_inverses(acc[0] - contract(x1b, lower_pair(0, 1)), LLI)
    for i in range(4):
        for q, packed in enumerate(pack(parts, slice(8 * i, 8 * i + 8))):
            s_last[i, q] = packed.astype(BF)
    for d in (4, 3, 5, 2, 6, 1, 7, 0):
        n = lax.rem(lax.rem(c, 8) + d, 8)
        copy_out(
            s_last.at[n // 2], r_last.at[z], top_ssem.at[7], top_rsem.at[7],
            {"col": 8 * h + n}, (c // 8 == h) if d == 0 else None,
        )
    out_send(0, x1)

    def own_rows(value):
        return jnp.where(h == 0, value[0:4], value[4:8])

    for copy in shared.values():
        copy.wait_send()
    for place in range(6):
        out_sent(place)
    await_bytes(r_last.at[pl.ds(0, 7)], top_ssem.at[7])

    @pl.when(h != c // 8)
    def _():
        await_bytes(r_last.at[7], top_ssem.at[7])

    await_bytes(r_out, out_rsem.at[0])
    for place in range(6):
        for k in range(4):
            value = own_rows(r_out[place, k // 2, k % 2])
            if place == 5:
                top[1, k] = value
            elif place == 4:
                top[0, k] = value
            else:
                sol[0, place + 1, k] = value
    await_bytes(r_last, top_rsem.at[7])
    for q in range(2):
        last = r_last[0, q].astype(F32)
        for zz in range(1, 8):
            last = last + r_last[zz, q].astype(F32)
        for i in range(2):
            sol[0, 0, 2 * q + i] = own_rows(last[8 * i : 8 * i + 8])


def on_device(
    right_side, top_right_side, leaf_upper, leaf_upper_mask, leaf_lower, leaf_lower_mask, cross_upper, cross_upper_mask,
    cross_lower, cross_lower_mask, top_upper, top_lower, leaf_upper_inverse, leaf_lower_inverse, top_upper_inverse,
    top_lower_inverse, leaf_sizes, top_sizes,
):
    in_hbm = pl.BlockSpec(memory_space=pl.ANY)
    in_smem = pl.BlockSpec(memory_space=pltpu.SMEM)
    in_vmem = pl.BlockSpec(memory_space=pltpu.VMEM)
    dma = pltpu.SemaphoreType.DMA
    return pl.pallas_call(
        kernel,
        out_shape=(
            jax.ShapeDtypeStruct((1, 5, 4, 4, 128), F32),
            jax.ShapeDtypeStruct((2, 4, 4, 128), F32),
        ),
        in_specs=[in_hbm] * 12 + [in_smem] * 6,
        out_specs=(in_vmem, in_vmem),
        scratch_shapes=[
            pltpu.VMEM((42, 2, 4, 128, 128), BF),
            pltpu.VMEM((14, 4, 128, 128), F32),
            pltpu.VMEM((14, 4, 128, 256), BF),
            pltpu.VMEM((5, 4, 32, 128), F32),
            pltpu.VMEM((2, 4, 32, 128), F32),
            pltpu.VMEM((7, 32, 512), F32),
            pltpu.VMEM((5, 32, 256), F32),
            pltpu.VMEM((32, 256), F32),
            pltpu.VMEM((5, 2, 2, 128, 128), BF),
            pltpu.VMEM((5, 4, 2, 128, 128), BF),
            pltpu.VMEM((4, 4, 32, 128), BF),
            pltpu.VMEM((4, 8, 4, 32, 128), BF),
            pltpu.VMEM((4, 2, 32, 128), BF),
            pltpu.VMEM((4, 4, 2, 32, 128), BF),
            pltpu.VMEM((4, 2, 2, 32, 128), BF),
            pltpu.VMEM((4, 8, 2, 32, 128), BF),
            pltpu.VMEM((5, 2, 32, 128), BF),
            pltpu.VMEM((2, 4, 2, 16, 128), F32),
            pltpu.VMEM((2, 4, 2, 16, 128), F32),
            pltpu.VMEM((2, 16, 128), BF),
            pltpu.VMEM((8, 16, 128), BF),
            pltpu.VMEM((2, 16, 128), BF),
            pltpu.VMEM((8, 2, 16, 128), BF),
            pltpu.VMEM((16, 128), BF),
            pltpu.VMEM((4, 16, 128), BF),
            pltpu.VMEM((4, 16, 128), F32),
            pltpu.VMEM((4, 16, 128), F32),
            pltpu.VMEM((4, 2, 16, 128), BF),
            pltpu.VMEM((8, 2, 16, 128), BF),
            pltpu.VMEM((6, 4, 2, 8, 128), F32),
            pltpu.VMEM((6, 2, 2, 8, 128), F32),
        ]
        + [dma((n,)) for n in (18, 8, 8, 4, 4, 4, 4, 4, 4, 5, 5, 5, 5, 5, 5, 8, 8, 6, 1)],
        compiler_params=pltpu.CompilerParams(
            collective_id=0, has_side_effects=True, vmem_limit_bytes=58 * 1024 * 1024
        ),
    )(
        right_side, top_right_side, leaf_upper, leaf_lower, cross_upper, cross_lower, top_upper, top_lower,
        leaf_upper_inverse, leaf_lower_inverse, top_upper_inverse, top_lower_inverse,
        leaf_upper_mask[0, :, 0].T, leaf_lower_mask[0, :, 0].T,
        cross_upper_mask[0, :, 0].transpose(1, 2, 0), cross_lower_mask[0, :, 0].transpose(0, 2, 1),
        leaf_sizes[0].T, top_sizes,
    )


def solution(mesh):
    in_specs = (
        P("rep", None, "row", None, None),
        P(None, "row", None, None),
        P("rep", None, "col", "row", None, None),
        P("rep", None, "col", "row"),
        P("rep", None, "col", "row", None, None),
        P("rep", None, "col", "row"),
        P("rep", None, "col", None, "row", None, None),
        P("rep", None, "col", None, "row"),
        P("rep", None, "col", None, "row", None, None),
        P("rep", None, "col", None, "row"),
        P(None, "col", "row", None, None),
        P(None, "col", "row", None, None),
        P("rep", None, "row", None, None),
        P("rep", None, "row", None, None),
        P(None, "row", None, None),
        P(None, "row", None, None),
        P("rep", None, "row"),
        P(None, "row"),
    )
    out_specs = (P("rep", None, "row", "col", None), P(None, "row", "col", None))
    return jax.shard_map(
        on_device, mesh=mesh, in_specs=in_specs, out_specs=out_specs, check_vma=False
    )
```

```python
import jax
import jax.numpy as jnp
from jax import lax
from jax.experimental import pallas as pl
from jax.experimental.pallas import tpu as pltpu
from jax.sharding import PartitionSpec as P

MESH = pl.DeviceIdType.MESH
BF = jnp.bfloat16
F32 = jnp.float32

LU, CU, CL, LL, TU, TL = 0, 10, 20, 30, 40, 41
LUI, LLI, TUI, TLI = 0, 5, 10, 12


def upper_pair(m, l):
    return LU + l * (l - 1) // 2 + m


def lower_pair(l, m):
    q = 4 - l
    return LL + q * (q - 1) // 2 + (m - l - 1)


TURNED = (
    (upper_pair(1, 2), LUI + 2),
    (upper_pair(3, 4), LUI + 4),
    (TL, TLI),
    (lower_pair(3, 4), LLI + 3),
    (lower_pair(1, 2), LLI + 1),
)


def kernel(
    rs, trs, lu, ll, cu, cl, tu, tl, lui, lli, tui, tli,
    lum, llm, cum, clm, ls, ts,
    sol, top,
    blk, inv_raw, inv, rhs, trhs, acc, y_keep, base,
    turn_out, relay, turn,
    s_z, r_z, s_x, r_x, s_zr, r_zr, r_d,
    s_cross, r_cross, s_top0, r_top0, s_mid, r_mid, r_low, xt1,
    s_last, r_last, s_out, r_out,
    load_sem, pair_ssem, pair_rsem, z_ssem, z_rsem, x_ssem, x_rsem, zr_ssem, zr_rsem, d_ssem, d_rsem,
    v_ssem, v_rsem, t_ssem, t_rsem, ts_ssem, ts_rsem, top_ssem, top_rsem, out_ssem, out_rsem,
):
    x = lax.axis_index("row")
    c = lax.axis_index("col")
    r = lax.axis_index("rep")
    z, h = c // 2, lax.rem(c, 2)
    even = lax.rem(z, 2) == 0
    first_k = 2 * lax.rem(z, 2)
    sibling = {"col": c + 1 - 2 * h}
    is_owner = (z // 2) == x
    owner = jnp.where(is_owner, 1.0, 0.0).astype(F32)
    low = jnp.where(z == 2 * x, 1.0, 0.0).astype(F32)
    high = jnp.where(z == 2 * x + 1, 1.0, 0.0).astype(F32)

    def row(d):
        return lax.rem(x + d, 4)

    def chip(d):
        return 2 * lax.rem(z + d, 8) + h

    half = pl.ds(pl.multiple_of(32 * h, 32), 32)
    loads = {}

    def load(name, src, dst):
        copy = pltpu.make_async_copy(src, dst, load_sem.at[len(loads)])
        copy.start()
        loads[name] = copy

    load("lui0", lui.at[0, pl.ds(0, 1)], inv_raw.at[pl.ds(LUI, 1)])
    load("rhs", rs.at[0, :, :, half], rhs)
    load("lu", lu.at[0, :, 0], blk.at[pl.ds(LU, 10), h])
    load("lui", lui.at[0, pl.ds(1, 4)], inv_raw.at[pl.ds(LUI + 1, 4)])
    for m in range(5):
        load(("cu", m), cu.at[0, m, 0], blk.at[pl.ds(CU + 2 * m, 2), h])
    load("trhs", trs.at[:, :, half], trhs)
    load("tui", tui, inv_raw.at[pl.ds(TUI, 2)])
    load("tli", tli, inv_raw.at[pl.ds(TLI, 2)])
    load("tu", tu.at[0], blk.at[pl.ds(TU, 1), h])
    load("tl", tl.at[0], blk.at[pl.ds(TL, 1), h])
    for a in range(2):
        load(("cl", a), cl.at[0, a, 0], blk.at[pl.ds(CL + 5 * a, 5), h])
    load("lli", lli.at[0], inv_raw.at[pl.ds(LLI, 5)])
    load("ll", ll.at[0, :, 0], blk.at[pl.ds(LL, 10), h])

    barrier = pltpu.get_barrier_semaphore()

    def greet(device):
        pl.semaphore_signal(barrier, inc=1, device_id=device, device_id_type=MESH)

    for d in (4, 3, 5, 2, 6, 1, 7):
        greet({"col": chip(d)})
    for d in (2, 1, 3):
        greet({"row": row(d)})
        greet({"rep": lax.rem(r + d, 4)})
    greet(sibling)

    def barrier_wait():
        pl.semaphore_wait(barrier, 14)

    def split(value):
        hi = value.astype(BF)
        return hi, (value - hi.astype(F32)).astype(BF)

    def masked_inverse(place, k, size):
        value = inv_raw[place, k]
        down = lax.broadcasted_iota(jnp.int32, (128, 128), 0)
        across = lax.broadcasted_iota(jnp.int32, (128, 128), 1)
        return jnp.where(jnp.maximum(down, across) < size, value, 0.0)

    def keep_inverse(place, k, value):
        hi, lo = split(value)
        inv[place, k, :, 0:128] = hi
        inv[place, k, :, 128:256] = lo

    def prepare_inverses(first, count, size_of):
        for i in range(count):
            for k in range(4):
                keep_inverse(first + i, k, masked_inverse(first + i, k, size_of(i, k)))

    def times_inverse(value, place, k):
        rows = value.shape[0]
        hi, lo = split(value)
        both = jnp.concatenate([hi, lo], axis=0)
        out = jnp.dot(both, inv[place, k], preferred_element_type=F32)
        return out[:rows, :128] + out[rows:, :128] + out[:rows, 128:]

    def cut(value):
        return [value[:, 128 * k : 128 * (k + 1)] for k in range(value.shape[1] // 128)]

    def apply_inverses(value, place):
        return [times_inverse(part, place, k) for k, part in enumerate(cut(value))]

    def own_pair_inverse(pair, place):
        return jnp.concatenate(
            [times_inverse(part, place, first_k + i) for i, part in enumerate(cut(pair))], axis=1
        )

    def contract(vectors, pair):
        columns = [
            jnp.concatenate([blk[pair, 0, k], blk[pair, 1, k]], axis=0) for k in range(4)
        ]
        return jnp.dot(vectors, jnp.concatenate(columns, axis=1), preferred_element_type=F32)

    def contract_turned(vectors, u):
        columns = [
            jnp.concatenate([turn[u, j, i] for j in range(4)], axis=0) for i in range(2)
        ]
        return jnp.dot(vectors, jnp.concatenate(columns, axis=1), preferred_element_type=F32)

    def mask_blocks(first, count, flag_of):
        def body(i, _):
            for k in range(4):
                flag = jnp.full((128, 128), flag_of(i, k).astype(F32), F32).astype(BF)
                blk[first + i, h, k] = blk[first + i, h, k] * flag
            return 0

        lax.fori_loop(0, count, body, 0)

    def remote_copy(src, dst, ssem, rsem, device):
        return pltpu.make_async_remote_copy(
            src_ref=src, dst_ref=dst, send_sem=ssem, recv_sem=rsem, device_id=device, device_id_type=MESH
        )

    def copy_out(src, dst, ssem, rsem, device, is_self=None):
        remote = remote_copy(src, dst, ssem, rsem, device)
        if is_self is None:
            remote.start()
            return

        @pl.when(is_self)
        def _():
            pltpu.make_async_copy(src, dst, rsem).start()

        @pl.when(jnp.logical_not(is_self))
        def _():
            remote.start()

    def await_bytes(ref, sem):
        pltpu.make_async_copy(ref, ref, sem).wait()

    shared = {}

    def share(name, first, count):
        at = len(shared)
        part = blk.at[pl.ds(first, count), h]
        copy = remote_copy(part, part, pair_ssem.at[at], pair_rsem.at[at], sibling)
        copy.start()
        shared[name] = copy

    def rows_of(source, level, scale):
        return jnp.concatenate([source[level, k] * scale for k in range(4)], axis=1)

    def owned(pair):
        return jnp.concatenate([pair * low, pair * high], axis=1)

    def own_pair(value):
        return jnp.where(even, value[:, :256], value[:, 256:])

    def turn_send(u):
        pair, place = TURNED[u]
        for k in range(4):
            out = jnp.dot(blk[pair, h, k], inv[place, k], preferred_element_type=F32)
            turn_out[u, k] = (out[:, :128] + out[:, 128:]).astype(BF)
        for d in (2, 1, 3):
            copy_out(turn_out.at[u, d], relay.at[u, x], v_ssem.at[u], v_rsem.at[u], {"row": row(d)})
        relay[u, x] = turn_out[u, 0]

    def turn_relay(u):
        await_bytes(relay.at[u, pl.ds(0, 3)], v_ssem.at[u])
        await_bytes(relay.at[u, pl.ds(0, 3)], v_rsem.at[u])
        for d in range(4):
            source = row(d)
            k = (4 - d) % 4
            copy_out(
                relay.at[u, source], turn.at[u, lax.rem(c, 4), k % 2], t_ssem.at[u], t_rsem.at[u],
                {"row": c // 4, "col": 4 * source + 2 * (k // 2) + h},
                (z == 2 * x) if d == 0 else None,
            )

    def turn_share(u):
        await_bytes(turn.at[u, pl.ds(0, 2)], t_rsem.at[u])
        await_bytes(relay.at[u, pl.ds(0, 3)], t_ssem.at[u])

        @pl.when(z != 2 * x)
        def _():
            await_bytes(relay.at[u, 3], t_ssem.at[u])

        for j in range(2):
            part = turn.at[u, 2 * j + h]
            remote_copy(part, part, ts_ssem.at[u], ts_rsem.at[u], sibling).start()

    def turn_ready(u):
        await_bytes(turn.at[u, pl.ds(0, 2)], ts_ssem.at[u])
        await_bytes(turn.at[u, pl.ds(0, 2)], ts_rsem.at[u])

    def z_send(step, parts):
        for k in range(4):
            s_z[step, k] = parts[k].astype(BF)
        for d in (4, 3, 5, 2, 6, 1, 7):
            copy_out(s_z.at[step], r_z.at[step, z], z_ssem.at[step], z_rsem.at[step], {"col": chip(d)})

    def z_receive(step, parts):
        await_bytes(r_z.at[step, pl.ds(0, 7)], z_ssem.at[step])
        await_bytes(r_z.at[step, pl.ds(0, 7)], z_rsem.at[step])
        totals = []
        for k in range(4):
            total = parts[k]
            for d in range(1, 8):
                total = total + r_z[step, lax.rem(z + d, 8), k].astype(F32)
            totals.append(total)
        return jnp.concatenate(totals, axis=1)

    def x_send(step, pair):
        for i, part in enumerate(cut(pair)):
            s_x[step, i] = part.astype(BF)
        for d in (2, 1, 3):
            copy_out(s_x.at[step], r_x.at[step, x], x_ssem.at[step], x_rsem.at[step], {"row": row(d)})

    def x_receive(step, pair):
        await_bytes(r_x.at[step, pl.ds(0, 3)], x_ssem.at[step])
        await_bytes(r_x.at[step, pl.ds(0, 3)], x_rsem.at[step])
        totals = []
        for i, total in enumerate(cut(pair)):
            for d in range(1, 4):
                total = total + r_x[step, row(d), i].astype(F32)
            totals.append(total)
        return jnp.concatenate(totals, axis=1)

    def gather_send(u, parts):
        for k in range(4):
            s_zr[u, k // 2, k % 2] = parts[k].astype(BF)
        for q in range(2):
            @pl.when(z != 2 * x + q)
            def _(q=q):
                copy_out(
                    s_zr.at[u, q], r_zr.at[u, z], zr_ssem.at[u], zr_rsem.at[u], {"col": 4 * x + 2 * q + h}
                )
        base[...] = own_pair(jnp.concatenate(parts, axis=1))

    def gather_receive(u):
        await_bytes(s_zr.at[u, 0], zr_ssem.at[u])

        @pl.when(jnp.logical_not(is_owner))
        def _():
            await_bytes(s_zr.at[u, 1], zr_ssem.at[u])
            base[...] = jnp.zeros_like(base)

        @pl.when(is_owner)
        def _():
            await_bytes(r_zr.at[u, pl.ds(0, 7)], zr_rsem.at[u])
            for i in range(2):
                total = base[:, 128 * i : 128 * (i + 1)]
                for d in range(1, 8):
                    total = total + r_zr[u, lax.rem(z + d, 8), i].astype(F32)
                base[:, 128 * i : 128 * (i + 1)] = total

    def spread_send(u, pair):
        @pl.when(is_owner)
        def _():
            for i, part in enumerate(cut(pair)):
                r_d[u, i] = part.astype(BF)
            for d in (2, 1, 3):
                copy_out(r_d.at[u], r_d.at[u], d_ssem.at[u], d_rsem.at[u], {"row": row(d)})

    def spread_receive(u):
        @pl.when(is_owner)
        def _():
            for d in range(3):
                await_bytes(r_d.at[u], d_ssem.at[u])

        @pl.when(jnp.logical_not(is_owner))
        def _():
            await_bytes(r_d.at[u], d_rsem.at[u])

        return jnp.concatenate([r_d[u, 0], r_d[u, 1]], axis=1)

    def pack(parts, rows):
        return [jnp.concatenate([parts[2 * q][rows], parts[2 * q + 1][rows]], axis=0) for q in range(2)]

    def unpack(value):
        return jnp.concatenate([value[:8], value[8:]], axis=1)

    def from_reps(quarters):
        return jnp.concatenate(
            [jnp.concatenate([quarter[8 * k : 8 * k + 8] for quarter in quarters], axis=0) for k in range(2)],
            axis=1,
        )

    def out_send(place, value):
        for i in range(4):
            for k in range(2):
                s_out[place, i, k] = value[8 * i : 8 * (i + 1), 128 * k : 128 * (k + 1)]

        @pl.when(is_owner)
        def _():
            for d in range(8):
                n = lax.rem(lax.rem(c, 8) + d, 8)
                copy_out(
                    s_out.at[place, n // 2], r_out.at[place, lax.rem(z, 2)],
                    out_ssem.at[place], out_rsem.at[0],
                    {"col": 8 * h + n}, (c // 8 == h) if d == 0 else None,
                )

    def out_sent(place):
        @pl.when(is_owner)
        def _():
            await_bytes(s_out.at[place], out_ssem.at[place])
            await_bytes(s_out.at[place, pl.ds(0, 3)], out_ssem.at[place])

            @pl.when(c // 8 != h)
            def _():
                await_bytes(s_out.at[place, 3], out_ssem.at[place])

    def subtract(level, vectors, pair):
        acc[level] = acc[level] - contract(vectors, pair)

    loads["lui0"].wait()
    prepare_inverses(LUI, 1, lambda i, k: ls[k, i])
    loads["rhs"].wait()
    y0 = own_pair_inverse(jnp.concatenate([rhs[0, first_k], rhs[0, first_k + 1]], axis=1), LUI)
    y_keep[0] = y0
    for l in range(1, 5):
        acc[l] = rows_of(rhs, l, 0.125)
    loads["lu"].wait()
    mask_blocks(LU, 10, lambda i, k: lum[k, i])
    loads["lui"].wait()
    prepare_inverses(LUI + 1, 4, lambda i, k: ls[k, i + 1])
    barrier_wait()

    spread_send(0, y0)
    for l in range(1, 5):
        share(("lu", l), upper_pair(0, l), l)
    turn_send(0)
    for m in range(5):
        loads["cu", m].wait()
        mask_blocks(CU + 2 * m, 2, lambda i, k, m=m: cum[i, k, m])
    share("cu", CU, 10)
    loads["trhs"].wait()
    for a in range(2):
        acc[5 + a] = rows_of(trhs, a, 0.03125)
    shared["lu", 1].wait_recv()
    y0b = spread_receive(0)

    parts = apply_inverses(acc[1] - contract(y0b, upper_pair(0, 1)), LUI + 1)
    z_send(0, parts)
    turn_relay(0)
    shared["lu", 2].wait_recv()
    gather_send(0, apply_inverses(acc[2] - contract(y0b, upper_pair(0, 2)), LUI + 2))
    shared["lu", 3].wait_recv()
    shared["lu", 4].wait_recv()
    for l in (3, 4):
        subtract(l, y0b, upper_pair(0, l))
    shared["cu"].wait_recv()
    for a in range(2):
        subtract(5 + a, y0b, CU + a)
    turn_send(1)
    turn_share(0)
    gather_receive(0)
    turn_ready(0)
    y1 = z_receive(0, parts)

    pair = base[...] - contract_turned(y1.astype(BF), 0)
    x_send(0, pair)
    own = own_pair(y1)
    y_keep[1] = own
    spread_send(1, own)
    turn_relay(1)
    y1b = spread_receive(1)
    subtract(3, y1b, upper_pair(1, 3))
    y2 = x_receive(0, pair)
    y_keep[2] = y2
    y2b = y2.astype(BF)

    parts = apply_inverses(acc[3] - contract(y2b, upper_pair(2, 3)), LUI + 3)
    z_send(1, parts)
    gather_send(
        1,
        apply_inverses(
            acc[4] - contract(y1b, upper_pair(1, 4)) - contract(y2b, upper_pair(2, 4)), LUI + 4
        ),
    )
    for a in range(2):
        acc[5 + a] = acc[5 + a] - contract(y1b, CU + 2 + a) - contract(y2b, CU + 4 + a)
    loads["tui"].wait()
    loads["tli"].wait()
    prepare_inverses(TUI, 1, lambda i, k: ts[i, k])
    prepare_inverses(TLI, 2, lambda i, k: ts[i, k])
    for k in range(4):
        upper = masked_inverse(TUI + 1, k, ts[1, k])
        keep_inverse(TUI + 1, k, times_inverse(upper, TLI + 1, k))
    turn_share(1)
    loads["lli"].wait()
    prepare_inverses(LLI, 5, lambda i, k: ls[k, i])
    loads["ll"].wait()
    mask_blocks(LL, 10, lambda i, k: llm[k, i])
    loads["tu"].wait()
    loads["tl"].wait()
    for u in (2, 3, 4):
        turn_send(u)
    gather_receive(1)
    turn_ready(1)
    y3 = z_receive(1, parts)

    pair = base[...] - contract_turned(y3.astype(BF), 1)
    x_send(1, pair)
    own = own_pair(y3)
    y_keep[3] = own
    spread_send(2, own)
    turn_relay(2)
    turn_relay(3)
    share("top", TU, 1)
    y3b = spread_receive(2)
    for a in range(2):
        subtract(5 + a, y3b, CU + 6 + a)
    y4 = x_receive(1, pair)
    y_keep[4] = y4
    y4b = y4.astype(BF)

    for a in range(2):
        parts = apply_inverses(acc[5 + a] - contract(y4b, CU + 8 + a), TUI + a)
        for rr in range(4):
            for q, packed in enumerate(pack(parts, slice(8 * rr, 8 * rr + 8))):
                s_cross[a, rr, q] = packed
        for e in (2, 1, 3):
            rr = lax.rem(r + e, 4)
            copy_out(
                s_cross.at[a, rr], r_cross.at[a, r], top_ssem.at[a], top_rsem.at[a], {"rep": rr}
            )
    turn_relay(4)
    for a in range(2):
        loads["cl", a].wait()
        mask_blocks(CL + 5 * a, 5, lambda i, k, a=a: clm[a, k, i])
    share("cl", CL, 10)

    def cross_receive(a):
        await_bytes(r_cross.at[a, pl.ds(0, 3)], top_ssem.at[a])
        await_bytes(r_cross.at[a, pl.ds(0, 3)], top_rsem.at[a])
        totals = []
        for q in range(2):
            total = s_cross[a, r, q]
            for e in range(1, 4):
                total = total + r_cross[a, lax.rem(r + e, 4), q]
            totals.append(total)
        return totals

    for q, packed in enumerate(cross_receive(0)):
        s_top0[q] = packed.astype(BF)
    for d in (2, 1, 3, 0):
        for q in range(2):
            copy_out(
                s_top0.at[q], r_top0.at[z], top_ssem.at[2], top_rsem.at[2],
                {"row": row(d), "col": 4 * x + 2 * q + h},
                (z == 2 * x + q) if d == 0 else None,
            )
    crossing = cross_receive(1)
    share("ll", LL, 10)
    for u in (2, 3, 4):
        turn_share(u)
    for u in (2, 3, 4):
        turn_ready(u)
    shared["top"].wait_recv()
    await_bytes(r_top0.at[pl.ds(0, 7)], top_ssem.at[2])

    @pl.when(jnp.logical_not(is_owner))
    def _():
        await_bytes(r_top0.at[7], top_ssem.at[2])

    await_bytes(r_top0, top_rsem.at[2])
    top0 = r_top0[0].astype(F32)
    for zz in range(1, 8):
        top0 = top0 + r_top0[zz].astype(F32)
    top0 = unpack(top0)

    parts = [-part for part in apply_inverses(contract(top0.astype(BF), TU), TUI + 1)]
    mine = [crossing[q] + packed for q, packed in enumerate(pack(parts, slice(0, 8)))]
    for q in range(2):
        s_mid[q] = mine[q].astype(BF)
    for d in (4, 3, 5, 2, 6, 1, 7):
        copy_out(s_mid, r_mid.at[z], top_ssem.at[3], top_rsem.at[3], {"col": chip(d)})
    top0_base = own_pair_inverse(top0, TLI) * owner
    await_bytes(r_mid.at[pl.ds(0, 7)], top_ssem.at[3])
    await_bytes(r_mid.at[pl.ds(0, 7)], top_rsem.at[3])
    for q in range(2):
        for d in range(1, 8):
            mine[q] = mine[q] + r_mid[lax.rem(z + d, 8), q].astype(F32)

    vectors = jnp.concatenate([unpack(mine[q]) for q in range(2)], axis=1).astype(BF)
    pair = top0_base - contract_turned(vectors, 2)
    here = 4 * r + x
    r_low[here] = jnp.concatenate(cut(pair), axis=0)
    for e in (2, 1, 3, 0):
        for d in (2, 1, 3, 0):
            if d or e:
                copy_out(
                    r_low.at[here], r_low.at[here], top_ssem.at[4], top_rsem.at[4],
                    {"row": row(d), "rep": lax.rem(r + e, 4)},
                )

    @pl.when(is_owner)
    def _():
        xt1[r] = jnp.where(even, mine[0], mine[1])
        for e in (2, 1, 3, 0):
            for d in (2, 1, 3, 0):
                if d or e:
                    copy_out(
                        xt1.at[r], xt1.at[r], top_ssem.at[6], top_rsem.at[6],
                        {"row": row(d), "rep": lax.rem(r + e, 4)},
                    )

    for l in range(5):
        acc[l] = owned(y_keep[l])
    @pl.when(is_owner)
    def _():
        for _ in range(5):
            await_bytes(xt1.at[pl.ds(0, 3)], top_ssem.at[6])
        await_bytes(xt1.at[pl.ds(0, 3)], top_rsem.at[6])

    @pl.when(jnp.logical_not(is_owner))
    def _():
        await_bytes(xt1, top_rsem.at[6])

    x_top1 = from_reps([xt1[rr] for rr in range(4)])
    xt1b = x_top1.astype(BF)
    shared["cl"].wait_recv()
    subtract(4, xt1b, CL + 9)
    await_bytes(r_low.at[pl.ds(0, 15)], top_ssem.at[4])
    await_bytes(r_low.at[pl.ds(0, 15)], top_rsem.at[4])
    x_top0 = from_reps([sum(r_low[4 * rr + xx] for xx in range(4)) for rr in range(4)])
    xt0b = x_top0.astype(BF)

    parts = apply_inverses(acc[4] - contract(xt0b, CL + 4), LLI + 4)
    z_send(2, parts)
    gather_send(
        2, apply_inverses(acc[3] - contract(xt1b, CL + 8) - contract(xt0b, CL + 3), LLI + 3)
    )
    out_send(5, x_top1)
    out_send(4, x_top0)
    for l in (2, 1, 0):
        acc[l] = acc[l] - contract(xt1b, CL + 5 + l) - contract(xt0b, CL + l)
    gather_receive(2)
    x4 = z_receive(2, parts)

    pair = base[...] - contract_turned(x4.astype(BF), 3)
    x_send(2, pair)
    own = own_pair(x4)
    spread_send(3, own)
    out_send(3, own)
    shared["ll"].wait_recv()
    x4b = spread_receive(3)
    subtract(2, x4b, lower_pair(2, 4))
    x3 = x_receive(2, pair)
    x3b = x3.astype(BF)

    parts = apply_inverses(acc[2] - contract(x3b, lower_pair(2, 3)), LLI + 2)
    z_send(3, parts)
    gather_send(
        3,
        apply_inverses(
            acc[1] - contract(x4b, lower_pair(1, 4)) - contract(x3b, lower_pair(1, 3)), LLI + 1
        ),
    )
    out_send(2, x3)
    acc[0] = acc[0] - contract(x4b, lower_pair(0, 4)) - contract(x3b, lower_pair(0, 3))
    gather_receive(3)
    x2 = z_receive(3, parts)

    pair = base[...] - contract_turned(x2.astype(BF), 4)
    x_send(3, pair)
    own = own_pair(x2)
    spread_send(4, own)
    out_send(1, own)
    x2b = spread_receive(4)
    subtract(0, x2b, lower_pair(0, 2))
    x1 = x_receive(3, pair)
    x1b = x1.astype(BF)

    parts = apply_inverses(acc[0] - contract(x1b, lower_pair(0, 1)), LLI)
    for i in range(4):
        for q, packed in enumerate(pack(parts, slice(8 * i, 8 * i + 8))):
            s_last[i, q] = packed.astype(BF)
    for d in (4, 3, 5, 2, 6, 1, 7, 0):
        n = lax.rem(lax.rem(c, 8) + d, 8)
        copy_out(
            s_last.at[n // 2], r_last.at[z], top_ssem.at[7], top_rsem.at[7],
            {"col": 8 * h + n}, (c // 8 == h) if d == 0 else None,
        )
    out_send(0, x1)

    def own_rows(value):
        return jnp.where(h == 0, value[0:4], value[4:8])

    for copy in shared.values():
        copy.wait_send()
    for place in range(6):
        out_sent(place)
    await_bytes(r_last.at[pl.ds(0, 7)], top_ssem.at[7])

    @pl.when(h != c // 8)
    def _():
        await_bytes(r_last.at[7], top_ssem.at[7])

    await_bytes(r_out, out_rsem.at[0])
    for place in range(6):
        for k in range(4):
            value = own_rows(r_out[place, k // 2, k % 2])
            if place == 5:
                top[1, k] = value
            elif place == 4:
                top[0, k] = value
            else:
                sol[0, place + 1, k] = value
    await_bytes(r_last, top_rsem.at[7])
    for q in range(2):
        last = r_last[0, q].astype(F32)
        for zz in range(1, 8):
            last = last + r_last[zz, q].astype(F32)
        for i in range(2):
            sol[0, 0, 2 * q + i] = own_rows(last[8 * i : 8 * i + 8])


def on_device(
    right_side, top_right_side, leaf_upper, leaf_upper_mask, leaf_lower, leaf_lower_mask, cross_upper, cross_upper_mask,
    cross_lower, cross_lower_mask, top_upper, top_lower, leaf_upper_inverse, leaf_lower_inverse, top_upper_inverse,
    top_lower_inverse, leaf_sizes, top_sizes,
):
    in_hbm = pl.BlockSpec(memory_space=pl.ANY)
    in_smem = pl.BlockSpec(memory_space=pltpu.SMEM)
    in_vmem = pl.BlockSpec(memory_space=pltpu.VMEM)
    dma = pltpu.SemaphoreType.DMA
    return pl.pallas_call(
        kernel,
        out_shape=(
            jax.ShapeDtypeStruct((1, 5, 4, 4, 128), F32),
            jax.ShapeDtypeStruct((2, 4, 4, 128), F32),
        ),
        in_specs=[in_hbm] * 12 + [in_smem] * 6,
        out_specs=(in_vmem, in_vmem),
        scratch_shapes=[
            pltpu.VMEM((42, 2, 4, 128, 128), BF),
            pltpu.VMEM((14, 4, 128, 128), F32),
            pltpu.VMEM((14, 4, 128, 256), BF),
            pltpu.VMEM((5, 4, 32, 128), F32),
            pltpu.VMEM((2, 4, 32, 128), F32),
            pltpu.VMEM((7, 32, 512), F32),
            pltpu.VMEM((5, 32, 256), F32),
            pltpu.VMEM((32, 256), F32),
            pltpu.VMEM((5, 4, 128, 128), BF),
            pltpu.VMEM((5, 4, 128, 128), BF),
            pltpu.VMEM((5, 4, 2, 128, 128), BF),
            pltpu.VMEM((4, 4, 32, 128), BF),
            pltpu.VMEM((4, 8, 4, 32, 128), BF),
            pltpu.VMEM((4, 2, 32, 128), BF),
            pltpu.VMEM((4, 4, 2, 32, 128), BF),
            pltpu.VMEM((4, 2, 2, 32, 128), BF),
            pltpu.VMEM((4, 8, 2, 32, 128), BF),
            pltpu.VMEM((5, 2, 32, 128), BF),
            pltpu.VMEM((2, 4, 2, 16, 128), F32),
            pltpu.VMEM((2, 4, 2, 16, 128), F32),
            pltpu.VMEM((2, 16, 128), BF),
            pltpu.VMEM((8, 16, 128), BF),
            pltpu.VMEM((2, 16, 128), BF),
            pltpu.VMEM((8, 2, 16, 128), BF),
            pltpu.VMEM((16, 16, 128), F32),
            pltpu.VMEM((4, 16, 128), F32),
            pltpu.VMEM((4, 2, 16, 128), BF),
            pltpu.VMEM((8, 2, 16, 128), BF),
            pltpu.VMEM((6, 4, 2, 8, 128), F32),
            pltpu.VMEM((6, 2, 2, 8, 128), F32),
        ]
        + [dma((n,)) for n in (18, 8, 8, 4, 4, 4, 4, 4, 4, 5, 5, 5, 5, 5, 5, 5, 5, 8, 8, 6, 1)],
        compiler_params=pltpu.CompilerParams(
            collective_id=0, has_side_effects=True, vmem_limit_bytes=58 * 1024 * 1024
        ),
    )(
        right_side, top_right_side, leaf_upper, leaf_lower, cross_upper, cross_lower, top_upper, top_lower,
        leaf_upper_inverse, leaf_lower_inverse, top_upper_inverse, top_lower_inverse,
        leaf_upper_mask[0, :, 0].T, leaf_lower_mask[0, :, 0].T,
        cross_upper_mask[0, :, 0].transpose(1, 2, 0), cross_lower_mask[0, :, 0].transpose(0, 2, 1),
        leaf_sizes[0].T, top_sizes,
    )


def solution(mesh):
    in_specs = (
        P("rep", None, "row", None, None),
        P(None, "row", None, None),
        P("rep", None, "col", "row", None, None),
        P("rep", None, "col", "row"),
        P("rep", None, "col", "row", None, None),
        P("rep", None, "col", "row"),
        P("rep", None, "col", None, "row", None, None),
        P("rep", None, "col", None, "row"),
        P("rep", None, "col", None, "row", None, None),
        P("rep", None, "col", None, "row"),
        P(None, "col", "row", None, None),
        P(None, "col", "row", None, None),
        P("rep", None, "row", None, None),
        P("rep", None, "row", None, None),
        P(None, "row", None, None),
        P(None, "row", None, None),
        P("rep", None, "row"),
        P(None, "row"),
    )
    out_specs = (P("rep", None, "row", "col", None), P(None, "row", "col", None))
    return jax.shard_map(
        on_device, mesh=mesh, in_specs=in_specs, out_specs=out_specs, check_vma=False
    )
```

```python
import jax
import jax.numpy as jnp
from jax import lax
from jax.experimental import pallas as pl
from jax.experimental.pallas import tpu as pltpu
from jax.sharding import PartitionSpec as P

MESH = pl.DeviceIdType.MESH
BF = jnp.bfloat16
F32 = jnp.float32

LU, CU, CL, LL, TU, TL = 0, 10, 20, 30, 40, 41
LUI, LLI, TUI, TLI = 0, 5, 10, 12


def upper_pair(m, l):
    return LU + l * (l - 1) // 2 + m


def lower_pair(l, m):
    q = 4 - l
    return LL + q * (q - 1) // 2 + (m - l - 1)


TURNED = (
    (upper_pair(1, 2), LUI + 2),
    (upper_pair(3, 4), LUI + 4),
    (TL, TLI),
    (lower_pair(3, 4), LLI + 3),
    (lower_pair(1, 2), LLI + 1),
)


def kernel(
    rs, trs, lu, ll, cu, cl, tu, tl, lui, lli, tui, tli,
    lum, llm, cum, clm, ls, ts,
    out,
    blk, inv_raw, inv, rhs, trhs, acc, y_keep, base,
    turn_out, relay, turn,
    s_z, r_z, s_x, r_x, s_zr, r_zr, r_d,
    s_cross, r_cross, s_top0, r_top0, s_mid, r_mid, r_low, xt1,
    s_last, r_last, s_out, r_out,
    load_sem, pair_ssem, pair_rsem, z_ssem, z_rsem, x_ssem, x_rsem, zr_ssem, zr_rsem, d_ssem, d_rsem,
    v_ssem, v_rsem, t_ssem, t_rsem, ts_ssem, ts_rsem, top_ssem, top_rsem, out_ssem, out_rsem,
):
    x = lax.axis_index("row")
    c = lax.axis_index("col")
    r = lax.axis_index("rep")
    z, h = c // 2, lax.rem(c, 2)
    even = lax.rem(z, 2) == 0
    first_k = 2 * lax.rem(z, 2)
    sibling = {"col": c + 1 - 2 * h}
    is_owner = (z // 2) == x
    owner = jnp.where(is_owner, 1.0, 0.0).astype(F32)
    low = jnp.where(z == 2 * x, 1.0, 0.0).astype(F32)
    high = jnp.where(z == 2 * x + 1, 1.0, 0.0).astype(F32)

    def row(d):
        return lax.rem(x + d, 4)

    def chip(d):
        return 2 * lax.rem(z + d, 8) + h

    half = pl.ds(pl.multiple_of(32 * h, 32), 32)
    loads = {}

    def load(name, src, dst):
        copy = pltpu.make_async_copy(src, dst, load_sem.at[len(loads)])
        copy.start()
        loads[name] = copy

    load("lui0", lui.at[0, pl.ds(0, 1)], inv_raw.at[pl.ds(LUI, 1)])
    load("rhs", rs.at[0, :, :, half], rhs)
    load("lu", lu.at[0, :, 0], blk.at[pl.ds(LU, 10), h])
    load("lui", lui.at[0, pl.ds(1, 4)], inv_raw.at[pl.ds(LUI + 1, 4)])
    for m in range(5):
        load(("cu", m), cu.at[0, m, 0], blk.at[pl.ds(CU + 2 * m, 2), h])
    load("trhs", trs.at[:, :, half], trhs)
    load("tui", tui, inv_raw.at[pl.ds(TUI, 2)])
    load("tli", tli, inv_raw.at[pl.ds(TLI, 2)])
    load("tu", tu.at[0], blk.at[pl.ds(TU, 1), h])
    load("tl", tl.at[0], blk.at[pl.ds(TL, 1), h])
    for a in range(2):
        load(("cl", a), cl.at[0, a, 0], blk.at[pl.ds(CL + 5 * a, 5), h])
    load("lli", lli.at[0], inv_raw.at[pl.ds(LLI, 5)])
    load("ll", ll.at[0, :, 0], blk.at[pl.ds(LL, 10), h])

    barrier = pltpu.get_barrier_semaphore()

    def greet(device):
        pl.semaphore_signal(barrier, inc=1, device_id=device, device_id_type=MESH)

    for d in (4, 3, 5, 2, 6, 1, 7):
        greet({"col": chip(d)})
    for d in (2, 1, 3):
        greet({"row": row(d)})
        greet({"rep": lax.rem(r + d, 4)})
    greet(sibling)

    def barrier_wait():
        pl.semaphore_wait(barrier, 14)

    def split(value):
        hi = value.astype(BF)
        return hi, (value - hi.astype(F32)).astype(BF)

    def masked_inverse(place, k, size):
        value = inv_raw[place, k]
        down = lax.broadcasted_iota(jnp.int32, (128, 128), 0)
        across = lax.broadcasted_iota(jnp.int32, (128, 128), 1)
        return jnp.where(jnp.maximum(down, across) < size, value, 0.0)

    def keep_inverse(place, k, value):
        hi, lo = split(value)
        inv[place, k, :, 0:128] = hi
        inv[place, k, :, 128:256] = lo

    def prepare_inverses(first, count, size_of):
        for i in range(count):
            for k in range(4):
                keep_inverse(first + i, k, masked_inverse(first + i, k, size_of(i, k)))

    def times_inverse(value, place, k):
        rows = value.shape[0]
        hi, lo = split(value)
        both = jnp.concatenate([hi, lo], axis=0)
        wide = jnp.dot(both, inv[place, k], preferred_element_type=F32)
        return wide[:rows, :128] + wide[rows:, :128] + wide[:rows, 128:]

    def cut(value):
        return [value[:, 128 * k : 128 * (k + 1)] for k in range(value.shape[1] // 128)]

    def apply_inverses(value, place):
        return [times_inverse(part, place, k) for k, part in enumerate(cut(value))]

    def own_pair_inverse(pair, place):
        return jnp.concatenate(
            [times_inverse(part, place, first_k + i) for i, part in enumerate(cut(pair))], axis=1
        )

    def contract(vectors, pair):
        columns = [
            jnp.concatenate([blk[pair, 0, k], blk[pair, 1, k]], axis=0) for k in range(4)
        ]
        return jnp.dot(vectors, jnp.concatenate(columns, axis=1), preferred_element_type=F32)

    def contract_turned(vectors, u):
        columns = [
            jnp.concatenate([turn[u, j, i] for j in range(4)], axis=0) for i in range(2)
        ]
        return jnp.dot(vectors, jnp.concatenate(columns, axis=1), preferred_element_type=F32)

    def mask_blocks(first, count, flag_of):
        def body(i, _):
            for k in range(4):
                flag = jnp.full((128, 128), flag_of(i, k).astype(F32), F32).astype(BF)
                blk[first + i, h, k] = blk[first + i, h, k] * flag
            return 0

        lax.fori_loop(0, count, body, 0)

    def remote_copy(src, dst, ssem, rsem, device):
        return pltpu.make_async_remote_copy(
            src_ref=src, dst_ref=dst, send_sem=ssem, recv_sem=rsem, device_id=device, device_id_type=MESH
        )

    def copy_out(src, dst, ssem, rsem, device, is_self=None):
        remote = remote_copy(src, dst, ssem, rsem, device)
        if is_self is None:
            remote.start()
            return

        @pl.when(is_self)
        def _():
            pltpu.make_async_copy(src, dst, rsem).start()

        @pl.when(jnp.logical_not(is_self))
        def _():
            remote.start()

    def await_bytes(ref, sem):
        pltpu.make_async_copy(ref, ref, sem).wait()

    shared = {}

    def share(name, first, count):
        at = len(shared)
        part = blk.at[pl.ds(first, count), h]
        copy = remote_copy(part, part, pair_ssem.at[at], pair_rsem.at[at], sibling)
        copy.start()
        shared[name] = copy

    def rows_of(source, level, scale):
        return jnp.concatenate([source[level, k] * scale for k in range(4)], axis=1)

    def owned(pair):
        return jnp.concatenate([pair * low, pair * high], axis=1)

    def own_pair(value):
        return jnp.where(even, value[:, :256], value[:, 256:])

    def turn_fold(u):
        pair, place = TURNED[u]
        for k in range(4):
            wide = jnp.dot(blk[pair, h, k], inv[place, k], preferred_element_type=F32)
            turn_out[u, k] = (wide[:, :128] + wide[:, 128:]).astype(BF)

    def turn_send(u):
        for d in (2, 1, 3):
            copy_out(turn_out.at[u, d], relay.at[u, x], v_ssem.at[u], v_rsem.at[u], {"row": row(d)})
        relay[u, x] = turn_out[u, 0]

    def turn_relay(u):
        await_bytes(relay.at[u, pl.ds(0, 3)], v_ssem.at[u])
        await_bytes(relay.at[u, pl.ds(0, 3)], v_rsem.at[u])
        for d in range(4):
            source = row(d)
            k = (4 - d) % 4
            copy_out(
                relay.at[u, source], turn.at[u, lax.rem(c, 4), k % 2], t_ssem.at[u], t_rsem.at[u],
                {"row": c // 4, "col": 4 * source + 2 * (k // 2) + h},
                (z == 2 * x) if d == 0 else None,
            )

    def turn_share(u):
        await_bytes(turn.at[u, pl.ds(0, 2)], t_rsem.at[u])
        await_bytes(relay.at[u, pl.ds(0, 3)], t_ssem.at[u])

        @pl.when(z != 2 * x)
        def _():
            await_bytes(relay.at[u, 3], t_ssem.at[u])

        for j in range(2):
            part = turn.at[u, 2 * j + h]
            remote_copy(part, part, ts_ssem.at[u], ts_rsem.at[u], sibling).start()

    def turn_ready(u):
        await_bytes(turn.at[u, pl.ds(0, 2)], ts_ssem.at[u])
        await_bytes(turn.at[u, pl.ds(0, 2)], ts_rsem.at[u])

    def z_send(step, parts):
        for k in range(4):
            s_z[step, k] = parts[k].astype(BF)
        for d in (4, 3, 5, 2, 6, 1, 7):
            copy_out(s_z.at[step], r_z.at[step, z], z_ssem.at[step], z_rsem.at[step], {"col": chip(d)})

    def z_receive(step, parts):
        await_bytes(r_z.at[step, pl.ds(0, 7)], z_ssem.at[step])
        await_bytes(r_z.at[step, pl.ds(0, 7)], z_rsem.at[step])
        totals = []
        for k in range(4):
            total = parts[k]
            for d in range(1, 8):
                total = total + r_z[step, lax.rem(z + d, 8), k].astype(F32)
            totals.append(total)
        return jnp.concatenate(totals, axis=1)

    def x_send(step, pair):
        for i, part in enumerate(cut(pair)):
            s_x[step, i] = part.astype(BF)
        for d in (2, 1, 3):
            copy_out(s_x.at[step], r_x.at[step, x], x_ssem.at[step], x_rsem.at[step], {"row": row(d)})

    def x_receive(step, pair):
        await_bytes(r_x.at[step, pl.ds(0, 3)], x_ssem.at[step])
        await_bytes(r_x.at[step, pl.ds(0, 3)], x_rsem.at[step])
        totals = []
        for i, total in enumerate(cut(pair)):
            for d in range(1, 4):
                total = total + r_x[step, row(d), i].astype(F32)
            totals.append(total)
        return jnp.concatenate(totals, axis=1)

    def gather_send(u, parts):
        for k in range(4):
            s_zr[u, k // 2, k % 2] = parts[k].astype(BF)
        for q in range(2):
            @pl.when(z != 2 * x + q)
            def _(q=q):
                copy_out(
                    s_zr.at[u, q], r_zr.at[u, z], zr_ssem.at[u], zr_rsem.at[u], {"col": 4 * x + 2 * q + h}
                )
        base[...] = own_pair(jnp.concatenate(parts, axis=1))

    def gather_receive(u):
        await_bytes(s_zr.at[u, 0], zr_ssem.at[u])

        @pl.when(jnp.logical_not(is_owner))
        def _():
            await_bytes(s_zr.at[u, 1], zr_ssem.at[u])
            base[...] = jnp.zeros_like(base)

        @pl.when(is_owner)
        def _():
            await_bytes(r_zr.at[u, pl.ds(0, 7)], zr_rsem.at[u])
            for i in range(2):
                total = base[:, 128 * i : 128 * (i + 1)]
                for d in range(1, 8):
                    total = total + r_zr[u, lax.rem(z + d, 8), i].astype(F32)
                base[:, 128 * i : 128 * (i + 1)] = total

    def spread_send(u, pair):
        @pl.when(is_owner)
        def _():
            for i, part in enumerate(cut(pair)):
                r_d[u, i] = part.astype(BF)
            for d in (2, 1, 3):
                copy_out(r_d.at[u], r_d.at[u], d_ssem.at[u], d_rsem.at[u], {"row": row(d)})

    def spread_receive(u):
        @pl.when(is_owner)
        def _():
            for d in range(3):
                await_bytes(r_d.at[u], d_ssem.at[u])

        @pl.when(jnp.logical_not(is_owner))
        def _():
            await_bytes(r_d.at[u], d_rsem.at[u])

        return jnp.concatenate([r_d[u, 0], r_d[u, 1]], axis=1)

    def pack(parts, rows):
        return [jnp.concatenate([parts[2 * q][rows], parts[2 * q + 1][rows]], axis=0) for q in range(2)]

    def unpack(value):
        return jnp.concatenate([value[:8], value[8:]], axis=1)

    def from_reps(quarters):
        return jnp.concatenate(
            [jnp.concatenate([quarter[8 * k : 8 * k + 8] for quarter in quarters], axis=0) for k in range(2)],
            axis=1,
        )

    def out_send(place, value):
        for i in range(4):
            for k in range(2):
                s_out[place, i, k] = value[8 * i : 8 * (i + 1), 128 * k : 128 * (k + 1)]

        @pl.when(is_owner)
        def _():
            for d in range(8):
                n = lax.rem(lax.rem(c, 8) + d, 8)
                copy_out(
                    s_out.at[place, n // 2], r_out.at[place, lax.rem(z, 2)],
                    out_ssem.at[place], out_rsem.at[0],
                    {"col": 8 * h + n}, (c // 8 == h) if d == 0 else None,
                )

    def out_sent(place):
        @pl.when(is_owner)
        def _():
            await_bytes(s_out.at[place], out_ssem.at[place])
            await_bytes(s_out.at[place, pl.ds(0, 3)], out_ssem.at[place])

            @pl.when(c // 8 != h)
            def _():
                await_bytes(s_out.at[place, 3], out_ssem.at[place])

    def subtract(level, vectors, pair):
        acc[level] = acc[level] - contract(vectors, pair)

    loads["lui0"].wait()
    prepare_inverses(LUI, 1, lambda i, k: ls[k, i])
    loads["rhs"].wait()
    y0 = own_pair_inverse(jnp.concatenate([rhs[0, first_k], rhs[0, first_k + 1]], axis=1), LUI)
    y_keep[0] = y0
    for l in range(1, 5):
        acc[l] = rows_of(rhs, l, 0.125)
    loads["lu"].wait()
    mask_blocks(LU, 10, lambda i, k: lum[k, i])
    loads["lui"].wait()
    prepare_inverses(LUI + 1, 4, lambda i, k: ls[k, i + 1])
    turn_fold(0)
    barrier_wait()

    spread_send(0, y0)
    turn_send(0)
    for l in range(1, 5):
        share(("lu", l), upper_pair(0, l), l)
    for m in range(5):
        loads["cu", m].wait()
        mask_blocks(CU + 2 * m, 2, lambda i, k, m=m: cum[i, k, m])
    share("cu", CU, 10)
    loads["trhs"].wait()
    for a in range(2):
        acc[5 + a] = rows_of(trhs, a, 0.03125)
    shared["lu", 1].wait_recv()
    y0b = spread_receive(0)

    parts = apply_inverses(acc[1] - contract(y0b, upper_pair(0, 1)), LUI + 1)
    z_send(0, parts)
    turn_relay(0)
    shared["lu", 2].wait_recv()
    gather_send(0, apply_inverses(acc[2] - contract(y0b, upper_pair(0, 2)), LUI + 2))
    shared["lu", 3].wait_recv()
    shared["lu", 4].wait_recv()
    for l in (3, 4):
        subtract(l, y0b, upper_pair(0, l))
    shared["cu"].wait_recv()
    for a in range(2):
        subtract(5 + a, y0b, CU + a)
    turn_fold(1)
    turn_send(1)
    turn_share(0)
    gather_receive(0)
    turn_ready(0)
    y1 = z_receive(0, parts)

    pair = base[...] - contract_turned(y1.astype(BF), 0)
    x_send(0, pair)
    own = own_pair(y1)
    y_keep[1] = own
    spread_send(1, own)
    turn_relay(1)
    y1b = spread_receive(1)
    subtract(3, y1b, upper_pair(1, 3))
    y2 = x_receive(0, pair)
    y_keep[2] = y2
    y2b = y2.astype(BF)

    parts = apply_inverses(acc[3] - contract(y2b, upper_pair(2, 3)), LUI + 3)
    z_send(1, parts)
    gather_send(
        1,
        apply_inverses(
            acc[4] - contract(y1b, upper_pair(1, 4)) - contract(y2b, upper_pair(2, 4)), LUI + 4
        ),
    )
    for a in range(2):
        acc[5 + a] = acc[5 + a] - contract(y1b, CU + 2 + a) - contract(y2b, CU + 4 + a)
    loads["tui"].wait()
    loads["tli"].wait()
    prepare_inverses(TUI, 1, lambda i, k: ts[i, k])
    prepare_inverses(TLI, 2, lambda i, k: ts[i, k])
    for k in range(4):
        upper = masked_inverse(TUI + 1, k, ts[1, k])
        keep_inverse(TUI + 1, k, times_inverse(upper, TLI + 1, k))
    turn_share(1)
    loads["lli"].wait()
    prepare_inverses(LLI, 5, lambda i, k: ls[k, i])
    loads["ll"].wait()
    mask_blocks(LL, 10, lambda i, k: llm[k, i])
    loads["tu"].wait()
    loads["tl"].wait()
    for u in (2, 3, 4):
        turn_fold(u)
        turn_send(u)
    gather_receive(1)
    turn_ready(1)
    y3 = z_receive(1, parts)

    pair = base[...] - contract_turned(y3.astype(BF), 1)
    x_send(1, pair)
    own = own_pair(y3)
    y_keep[3] = own
    spread_send(2, own)
    turn_relay(2)
    turn_relay(3)
    share("top", TU, 1)
    y3b = spread_receive(2)
    for a in range(2):
        subtract(5 + a, y3b, CU + 6 + a)
    y4 = x_receive(1, pair)
    y_keep[4] = y4
    y4b = y4.astype(BF)

    for a in range(2):
        parts = apply_inverses(acc[5 + a] - contract(y4b, CU + 8 + a), TUI + a)
        for rr in range(4):
            for q, packed in enumerate(pack(parts, slice(8 * rr, 8 * rr + 8))):
                s_cross[a, rr, q] = packed
        for e in (2, 1, 3):
            rr = lax.rem(r + e, 4)
            copy_out(
                s_cross.at[a, rr], r_cross.at[a, r], top_ssem.at[a], top_rsem.at[a], {"rep": rr}
            )
    turn_relay(4)
    for a in range(2):
        loads["cl", a].wait()
        mask_blocks(CL + 5 * a, 5, lambda i, k, a=a: clm[a, k, i])
    share("cl", CL, 10)

    def cross_receive(a):
        await_bytes(r_cross.at[a, pl.ds(0, 3)], top_ssem.at[a])
        await_bytes(r_cross.at[a, pl.ds(0, 3)], top_rsem.at[a])
        totals = []
        for q in range(2):
            total = s_cross[a, r, q]
            for e in range(1, 4):
                total = total + r_cross[a, lax.rem(r + e, 4), q]
            totals.append(total)
        return totals

    for q, packed in enumerate(cross_receive(0)):
        s_top0[q] = packed.astype(BF)
    for d in (2, 1, 3, 0):
        for q in range(2):
            copy_out(
                s_top0.at[q], r_top0.at[z], top_ssem.at[2], top_rsem.at[2],
                {"row": row(d), "col": 4 * x + 2 * q + h},
                (z == 2 * x + q) if d == 0 else None,
            )
    crossing = cross_receive(1)
    share("ll", LL, 10)
    turn_share(2)
    turn_share(3)
    turn_ready(2)
    shared["top"].wait_recv()
    await_bytes(r_top0.at[pl.ds(0, 7)], top_ssem.at[2])

    @pl.when(jnp.logical_not(is_owner))
    def _():
        await_bytes(r_top0.at[7], top_ssem.at[2])

    await_bytes(r_top0, top_rsem.at[2])
    top0 = r_top0[0].astype(F32)
    for zz in range(1, 8):
        top0 = top0 + r_top0[zz].astype(F32)
    top0 = unpack(top0)

    parts = [-part for part in apply_inverses(contract(top0.astype(BF), TU), TUI + 1)]
    mine = [crossing[q] + packed for q, packed in enumerate(pack(parts, slice(0, 8)))]
    for q in range(2):
        s_mid[q] = mine[q].astype(BF)
    for d in (4, 3, 5, 2, 6, 1, 7):
        copy_out(s_mid, r_mid.at[z], top_ssem.at[3], top_rsem.at[3], {"col": chip(d)})
    top0_base = own_pair_inverse(top0, TLI) * owner
    await_bytes(r_mid.at[pl.ds(0, 7)], top_ssem.at[3])
    await_bytes(r_mid.at[pl.ds(0, 7)], top_rsem.at[3])
    for q in range(2):
        for d in range(1, 8):
            mine[q] = mine[q] + r_mid[lax.rem(z + d, 8), q].astype(F32)

    vectors = jnp.concatenate([unpack(mine[q]) for q in range(2)], axis=1).astype(BF)
    pair = top0_base - contract_turned(vectors, 2)
    here = 4 * r + x
    r_low[here] = jnp.concatenate(cut(pair), axis=0)
    for e in (2, 1, 3, 0):
        for d in (2, 1, 3, 0):
            if d or e:
                copy_out(
                    r_low.at[here], r_low.at[here], top_ssem.at[4], top_rsem.at[4],
                    {"row": row(d), "rep": lax.rem(r + e, 4)},
                )

    @pl.when(is_owner)
    def _():
        xt1[r] = jnp.where(even, mine[0], mine[1])
        for e in (2, 1, 3, 0):
            for d in (2, 1, 3, 0):
                if d or e:
                    copy_out(
                        xt1.at[r], xt1.at[r], top_ssem.at[6], top_rsem.at[6],
                        {"row": row(d), "rep": lax.rem(r + e, 4)},
                    )

    for l in range(5):
        acc[l] = owned(y_keep[l])
    @pl.when(is_owner)
    def _():
        for _ in range(5):
            await_bytes(xt1.at[pl.ds(0, 3)], top_ssem.at[6])
        await_bytes(xt1.at[pl.ds(0, 3)], top_rsem.at[6])

    @pl.when(jnp.logical_not(is_owner))
    def _():
        await_bytes(xt1, top_rsem.at[6])

    x_top1 = from_reps([xt1[rr] for rr in range(4)])
    xt1b = x_top1.astype(BF)
    shared["cl"].wait_recv()
    subtract(4, xt1b, CL + 9)
    await_bytes(r_low.at[pl.ds(0, 15)], top_ssem.at[4])
    await_bytes(r_low.at[pl.ds(0, 15)], top_rsem.at[4])
    x_top0 = from_reps([sum(r_low[4 * rr + xx] for xx in range(4)) for rr in range(4)])
    xt0b = x_top0.astype(BF)

    parts = apply_inverses(acc[4] - contract(xt0b, CL + 4), LLI + 4)
    z_send(2, parts)
    gather_send(
        2, apply_inverses(acc[3] - contract(xt1b, CL + 8) - contract(xt0b, CL + 3), LLI + 3)
    )
    out_send(5, x_top1)
    out_send(4, x_top0)
    for l in (2, 1, 0):
        acc[l] = acc[l] - contract(xt1b, CL + 5 + l) - contract(xt0b, CL + l)
    turn_share(4)
    gather_receive(2)
    turn_ready(3)
    x4 = z_receive(2, parts)

    pair = base[...] - contract_turned(x4.astype(BF), 3)
    x_send(2, pair)
    own = own_pair(x4)
    spread_send(3, own)
    out_send(3, own)
    shared["ll"].wait_recv()
    x4b = spread_receive(3)
    subtract(2, x4b, lower_pair(2, 4))
    x3 = x_receive(2, pair)
    x3b = x3.astype(BF)

    parts = apply_inverses(acc[2] - contract(x3b, lower_pair(2, 3)), LLI + 2)
    z_send(3, parts)
    gather_send(
        3,
        apply_inverses(
            acc[1] - contract(x4b, lower_pair(1, 4)) - contract(x3b, lower_pair(1, 3)), LLI + 1
        ),
    )
    out_send(2, x3)
    acc[0] = acc[0] - contract(x4b, lower_pair(0, 4)) - contract(x3b, lower_pair(0, 3))
    turn_ready(4)
    gather_receive(3)
    x2 = z_receive(3, parts)

    pair = base[...] - contract_turned(x2.astype(BF), 4)
    x_send(3, pair)
    own = own_pair(x2)
    spread_send(4, own)
    out_send(1, own)
    x2b = spread_receive(4)
    subtract(0, x2b, lower_pair(0, 2))
    x1 = x_receive(3, pair)
    x1b = x1.astype(BF)

    parts = apply_inverses(acc[0] - contract(x1b, lower_pair(0, 1)), LLI)
    for i in range(4):
        for q, packed in enumerate(pack(parts, slice(8 * i, 8 * i + 8))):
            s_last[i, q] = packed.astype(BF)
    for d in (4, 3, 5, 2, 6, 1, 7, 0):
        n = lax.rem(lax.rem(c, 8) + d, 8)
        copy_out(
            s_last.at[n // 2], r_last.at[z], top_ssem.at[7], top_rsem.at[7],
            {"col": 8 * h + n}, (c // 8 == h) if d == 0 else None,
        )
    out_send(0, x1)

    def own_rows(value):
        return jnp.where(h == 0, value[0:4], value[4:8])

    for copy in shared.values():
        copy.wait_send()
    for place in range(6):
        out_sent(place)
    await_bytes(r_last.at[pl.ds(0, 7)], top_ssem.at[7])

    @pl.when(h != c // 8)
    def _():
        await_bytes(r_last.at[7], top_ssem.at[7])

    await_bytes(r_out, out_rsem.at[0])
    for place in range(6):
        for k in range(4):
            value = own_rows(r_out[place, k // 2, k % 2])
            if place == 5:
                out[6, k] = value
            elif place == 4:
                out[5, k] = value
            else:
                out[place + 1, k] = value
    await_bytes(r_last, top_rsem.at[7])
    for q in range(2):
        last = r_last[0, q].astype(F32)
        for zz in range(1, 8):
            last = last + r_last[zz, q].astype(F32)
        for i in range(2):
            out[0, 2 * q + i] = own_rows(last[8 * i : 8 * i + 8])


def on_device(
    right_side, top_right_side, leaf_upper, leaf_upper_mask, leaf_lower, leaf_lower_mask, cross_upper, cross_upper_mask,
    cross_lower, cross_lower_mask, top_upper, top_lower, leaf_upper_inverse, leaf_lower_inverse, top_upper_inverse,
    top_lower_inverse, leaf_sizes, top_sizes,
):
    in_hbm = pl.BlockSpec(memory_space=pl.ANY)
    in_smem = pl.BlockSpec(memory_space=pltpu.SMEM)
    in_vmem = pl.BlockSpec(memory_space=pltpu.VMEM)
    dma = pltpu.SemaphoreType.DMA
    out = pl.pallas_call(
        kernel,
        out_shape=jax.ShapeDtypeStruct((7, 4, 4, 128), F32),
        in_specs=[in_hbm] * 12 + [in_smem] * 6,
        out_specs=in_vmem,
        scratch_shapes=[
            pltpu.VMEM((42, 2, 4, 128, 128), BF),
            pltpu.VMEM((14, 4, 128, 128), F32),
            pltpu.VMEM((14, 4, 128, 256), BF),
            pltpu.VMEM((5, 4, 32, 128), F32),
            pltpu.VMEM((2, 4, 32, 128), F32),
            pltpu.VMEM((7, 32, 512), F32),
            pltpu.VMEM((5, 32, 256), F32),
            pltpu.VMEM((32, 256), F32),
            pltpu.VMEM((5, 4, 128, 128), BF),
            pltpu.VMEM((5, 4, 128, 128), BF),
            pltpu.VMEM((5, 4, 2, 128, 128), BF),
            pltpu.VMEM((4, 4, 32, 128), BF),
            pltpu.VMEM((4, 8, 4, 32, 128), BF),
            pltpu.VMEM((4, 2, 32, 128), BF),
            pltpu.VMEM((4, 4, 2, 32, 128), BF),
            pltpu.VMEM((4, 2, 2, 32, 128), BF),
            pltpu.VMEM((4, 8, 2, 32, 128), BF),
            pltpu.VMEM((5, 2, 32, 128), BF),
            pltpu.VMEM((2, 4, 2, 16, 128), F32),
            pltpu.VMEM((2, 4, 2, 16, 128), F32),
            pltpu.VMEM((2, 16, 128), BF),
            pltpu.VMEM((8, 16, 128), BF),
            pltpu.VMEM((2, 16, 128), BF),
            pltpu.VMEM((8, 2, 16, 128), BF),
            pltpu.VMEM((16, 16, 128), F32),
            pltpu.VMEM((4, 16, 128), F32),
            pltpu.VMEM((4, 2, 16, 128), BF),
            pltpu.VMEM((8, 2, 16, 128), BF),
            pltpu.VMEM((6, 4, 2, 8, 128), F32),
            pltpu.VMEM((6, 2, 2, 8, 128), F32),
        ]
        + [dma((n,)) for n in (18, 8, 8, 4, 4, 4, 4, 4, 4, 5, 5, 5, 5, 5, 5, 5, 5, 8, 8, 6, 1)],
        compiler_params=pltpu.CompilerParams(
            collective_id=0, has_side_effects=True, vmem_limit_bytes=58 * 1024 * 1024
        ),
    )(
        right_side, top_right_side, leaf_upper, leaf_lower, cross_upper, cross_lower, top_upper, top_lower,
        leaf_upper_inverse, leaf_lower_inverse, top_upper_inverse, top_lower_inverse,
        leaf_upper_mask[0, :, 0].T, leaf_lower_mask[0, :, 0].T,
        cross_upper_mask[0, :, 0].transpose(1, 2, 0), cross_lower_mask[0, :, 0].transpose(0, 2, 1),
        leaf_sizes[0].T, top_sizes,
    )
    return out[None, :5], out[5:]


def solution(mesh):
    in_specs = (
        P("rep", None, "row", None, None),
        P(None, "row", None, None),
        P("rep", None, "col", "row", None, None),
        P("rep", None, "col", "row"),
        P("rep", None, "col", "row", None, None),
        P("rep", None, "col", "row"),
        P("rep", None, "col", None, "row", None, None),
        P("rep", None, "col", None, "row"),
        P("rep", None, "col", None, "row", None, None),
        P("rep", None, "col", None, "row"),
        P(None, "col", "row", None, None),
        P(None, "col", "row", None, None),
        P("rep", None, "row", None, None),
        P("rep", None, "row", None, None),
        P(None, "row", None, None),
        P(None, "row", None, None),
        P("rep", None, "row"),
        P(None, "row"),
    )
    out_specs = (P("rep", None, "row", "col", None), P(None, "row", "col", None))
    return jax.shard_map(
        on_device, mesh=mesh, in_specs=in_specs, out_specs=out_specs, check_vma=False
    )
```

```python
import jax
import jax.numpy as jnp
from jax import lax
from jax.experimental import pallas as pl
from jax.experimental.pallas import tpu as pltpu
from jax.sharding import PartitionSpec as P

MESH = pl.DeviceIdType.MESH
BF = jnp.bfloat16
F32 = jnp.float32

LU, CU, CL, LL, TU, TL = 0, 10, 20, 30, 40, 41
LUI, LLI, TUI, TLI = 0, 5, 10, 12


def upper_pair(m, l):
    return LU + l * (l - 1) // 2 + m


def lower_pair(l, m):
    q = 4 - l
    return LL + q * (q - 1) // 2 + (m - l - 1)


TURNED = (
    (upper_pair(1, 2), LUI + 2),
    (upper_pair(3, 4), LUI + 4),
    (TL, TLI),
    (lower_pair(3, 4), LLI + 3),
    (lower_pair(1, 2), LLI + 1),
)


def kernel(
    rs, trs, lu, ll, cu, cl, tu, tl, lui, lli, tui, tli,
    lum, llm, cum, clm, ls, ts,
    out,
    blk, inv_raw, inv, rhs, trhs, acc, y_keep, base,
    turn_out, relay, turn,
    s_z, r_z, s_x, r_x, s_zr, r_zr, r_d,
    s_cross, r_cross, s_top0, r_top0, s_mid, r_mid, r_low, xt1,
    s_last, r_last, s_out, r_out,
    load_sem, pair_ssem, pair_rsem, z_ssem, z_rsem, x_ssem, x_rsem, zr_ssem, zr_rsem, d_ssem, d_rsem,
    v_ssem, v_rsem, t_ssem, t_rsem, ts_ssem, ts_rsem, top_ssem, top_rsem, out_ssem, out_rsem,
):
    x = lax.axis_index("row")
    c = lax.axis_index("col")
    r = lax.axis_index("rep")
    z, h = c // 2, lax.rem(c, 2)
    even = lax.rem(z, 2) == 0
    first_k = 2 * lax.rem(z, 2)
    sibling = {"col": c + 1 - 2 * h}
    is_owner = (z // 2) == x
    owner = jnp.where(is_owner, 1.0, 0.0).astype(F32)
    low = jnp.where(z == 2 * x, 1.0, 0.0).astype(F32)
    high = jnp.where(z == 2 * x + 1, 1.0, 0.0).astype(F32)

    def row(d):
        return lax.rem(x + d, 4)

    def chip(d):
        return 2 * lax.rem(z + d, 8) + h

    half = pl.ds(pl.multiple_of(32 * h, 32), 32)
    loads = {}

    def load(name, src, dst):
        copy = pltpu.make_async_copy(src, dst, load_sem.at[len(loads)])
        copy.start()
        loads[name] = copy

    load("lui0", lui.at[0, pl.ds(0, 1)], inv_raw.at[pl.ds(LUI, 1)])
    load("rhs", rs.at[0, :, :, half], rhs)
    load("lu", lu.at[0, pl.ds(0, 3), 0], blk.at[pl.ds(LU, 3), h])
    load("lui", lui.at[0, pl.ds(1, 2)], inv_raw.at[pl.ds(LUI + 1, 2)])
    load("lu later", lu.at[0, pl.ds(3, 7), 0], blk.at[pl.ds(LU + 3, 7), h])
    load("lui later", lui.at[0, pl.ds(3, 2)], inv_raw.at[pl.ds(LUI + 3, 2)])
    for m in range(5):
        load(("cu", m), cu.at[0, m, 0], blk.at[pl.ds(CU + 2 * m, 2), h])
    load("trhs", trs.at[:, :, half], trhs)
    load("tui", tui, inv_raw.at[pl.ds(TUI, 2)])
    load("tli", tli, inv_raw.at[pl.ds(TLI, 2)])
    load("tu", tu.at[0], blk.at[pl.ds(TU, 1), h])
    load("tl", tl.at[0], blk.at[pl.ds(TL, 1), h])
    for a in range(2):
        load(("cl", a), cl.at[0, a, 0], blk.at[pl.ds(CL + 5 * a, 5), h])
    load("lli", lli.at[0], inv_raw.at[pl.ds(LLI, 5)])
    load("ll", ll.at[0, :, 0], blk.at[pl.ds(LL, 10), h])

    barrier = pltpu.get_barrier_semaphore()

    def greet(device):
        pl.semaphore_signal(barrier, inc=1, device_id=device, device_id_type=MESH)

    for d in (4, 3, 5, 2, 6, 1, 7):
        greet({"col": chip(d)})
    for d in (2, 1, 3):
        greet({"row": row(d)})
        greet({"rep": lax.rem(r + d, 4)})
    greet(sibling)

    def barrier_wait():
        pl.semaphore_wait(barrier, 14)

    def split(value):
        hi = value.astype(BF)
        return hi, (value - hi.astype(F32)).astype(BF)

    def masked_inverse(place, k, size):
        value = inv_raw[place, k]
        down = lax.broadcasted_iota(jnp.int32, (128, 128), 0)
        across = lax.broadcasted_iota(jnp.int32, (128, 128), 1)
        return jnp.where(jnp.maximum(down, across) < size, value, 0.0)

    def keep_inverse(place, k, value):
        hi, lo = split(value)
        inv[place, k, :, 0:128] = hi
        inv[place, k, :, 128:256] = lo

    def prepare_inverses(first, count, size_of):
        for i in range(count):
            for k in range(4):
                keep_inverse(first + i, k, masked_inverse(first + i, k, size_of(i, k)))

    def times_inverse(value, place, k):
        rows = value.shape[0]
        hi, lo = split(value)
        both = jnp.concatenate([hi, lo], axis=0)
        wide = jnp.dot(both, inv[place, k], preferred_element_type=F32)
        return wide[:rows, :128] + wide[rows:, :128] + wide[:rows, 128:]

    def cut(value):
        return [value[:, 128 * k : 128 * (k + 1)] for k in range(value.shape[1] // 128)]

    def apply_inverses(value, place):
        return [times_inverse(part, place, k) for k, part in enumerate(cut(value))]

    def own_pair_inverse(pair, place):
        return jnp.concatenate(
            [times_inverse(part, place, first_k + i) for i, part in enumerate(cut(pair))], axis=1
        )

    def contract(vectors, pair):
        columns = [
            jnp.concatenate([blk[pair, 0, k], blk[pair, 1, k]], axis=0) for k in range(4)
        ]
        return jnp.dot(vectors, jnp.concatenate(columns, axis=1), preferred_element_type=F32)

    def contract_turned(vectors, u):
        columns = [
            jnp.concatenate([turn[u, j, i] for j in range(4)], axis=0) for i in range(2)
        ]
        return jnp.dot(vectors, jnp.concatenate(columns, axis=1), preferred_element_type=F32)

    def mask_blocks(first, count, flag_of):
        def body(i, _):
            for k in range(4):
                flag = jnp.full((128, 128), flag_of(i, k).astype(F32), F32).astype(BF)
                blk[first + i, h, k] = blk[first + i, h, k] * flag
            return 0

        lax.fori_loop(0, count, body, 0)

    def remote_copy(src, dst, ssem, rsem, device):
        return pltpu.make_async_remote_copy(
            src_ref=src, dst_ref=dst, send_sem=ssem, recv_sem=rsem, device_id=device, device_id_type=MESH
        )

    def copy_out(src, dst, ssem, rsem, device, is_self=None):
        remote = remote_copy(src, dst, ssem, rsem, device)
        if is_self is None:
            remote.start()
            return

        @pl.when(is_self)
        def _():
            pltpu.make_async_copy(src, dst, rsem).start()

        @pl.when(jnp.logical_not(is_self))
        def _():
            remote.start()

    def await_bytes(ref, sem):
        pltpu.make_async_copy(ref, ref, sem).wait()

    shared = {}

    def share(name, first, count):
        at = len(shared)
        part = blk.at[pl.ds(first, count), h]
        copy = remote_copy(part, part, pair_ssem.at[at], pair_rsem.at[at], sibling)
        copy.start()
        shared[name] = copy

    def rows_of(source, level, scale):
        return jnp.concatenate([source[level, k] * scale for k in range(4)], axis=1)

    def owned(pair):
        return jnp.concatenate([pair * low, pair * high], axis=1)

    def own_pair(value):
        return jnp.where(even, value[:, :256], value[:, 256:])

    def turn_fold(u):
        pair, place = TURNED[u]
        for k in range(4):
            wide = jnp.dot(blk[pair, h, k], inv[place, k], preferred_element_type=F32)
            turn_out[u, k] = (wide[:, :128] + wide[:, 128:]).astype(BF)

    def turn_send(u):
        for d in (2, 1, 3):
            copy_out(turn_out.at[u, d], relay.at[u, x], v_ssem.at[u], v_rsem.at[u], {"row": row(d)})
        relay[u, x] = turn_out[u, 0]

    def turn_relay(u):
        await_bytes(relay.at[u, pl.ds(0, 3)], v_ssem.at[u])
        await_bytes(relay.at[u, pl.ds(0, 3)], v_rsem.at[u])
        for d in range(4):
            source = row(d)
            k = (4 - d) % 4
            copy_out(
                relay.at[u, source], turn.at[u, lax.rem(c, 4), k % 2], t_ssem.at[u], t_rsem.at[u],
                {"row": c // 4, "col": 4 * source + 2 * (k // 2) + h},
                (z == 2 * x) if d == 0 else None,
            )

    def turn_share(u):
        await_bytes(turn.at[u, pl.ds(0, 2)], t_rsem.at[u])
        await_bytes(relay.at[u, pl.ds(0, 3)], t_ssem.at[u])

        @pl.when(z != 2 * x)
        def _():
            await_bytes(relay.at[u, 3], t_ssem.at[u])

        for j in range(2):
            part = turn.at[u, 2 * j + h]
            remote_copy(part, part, ts_ssem.at[u], ts_rsem.at[u], sibling).start()

    def turn_ready(u):
        await_bytes(turn.at[u, pl.ds(0, 2)], ts_ssem.at[u])
        await_bytes(turn.at[u, pl.ds(0, 2)], ts_rsem.at[u])

    def z_send(step, parts):
        for k in range(4):
            s_z[step, k] = parts[k].astype(BF)
        for d in (4, 3, 5, 2, 6, 1, 7):
            copy_out(s_z.at[step], r_z.at[step, z], z_ssem.at[step], z_rsem.at[step], {"col": chip(d)})

    def z_receive(step, parts):
        await_bytes(r_z.at[step, pl.ds(0, 7)], z_ssem.at[step])
        await_bytes(r_z.at[step, pl.ds(0, 7)], z_rsem.at[step])
        totals = []
        for k in range(4):
            total = parts[k]
            for d in range(1, 8):
                total = total + r_z[step, lax.rem(z + d, 8), k].astype(F32)
            totals.append(total)
        return jnp.concatenate(totals, axis=1)

    def x_send(step, pair):
        for i, part in enumerate(cut(pair)):
            s_x[step, i] = part.astype(BF)
        for d in (2, 1, 3):
            copy_out(s_x.at[step], r_x.at[step, x], x_ssem.at[step], x_rsem.at[step], {"row": row(d)})

    def x_receive(step, pair):
        await_bytes(r_x.at[step, pl.ds(0, 3)], x_ssem.at[step])
        await_bytes(r_x.at[step, pl.ds(0, 3)], x_rsem.at[step])
        totals = []
        for i, total in enumerate(cut(pair)):
            for d in range(1, 4):
                total = total + r_x[step, row(d), i].astype(F32)
            totals.append(total)
        return jnp.concatenate(totals, axis=1)

    def gather_send(u, parts):
        for k in range(4):
            s_zr[u, k // 2, k % 2] = parts[k].astype(BF)
        for q in range(2):
            @pl.when(z != 2 * x + q)
            def _(q=q):
                copy_out(
                    s_zr.at[u, q], r_zr.at[u, z], zr_ssem.at[u], zr_rsem.at[u], {"col": 4 * x + 2 * q + h}
                )
        base[...] = own_pair(jnp.concatenate(parts, axis=1))

    def gather_receive(u):
        await_bytes(s_zr.at[u, 0], zr_ssem.at[u])

        @pl.when(jnp.logical_not(is_owner))
        def _():
            await_bytes(s_zr.at[u, 1], zr_ssem.at[u])
            base[...] = jnp.zeros_like(base)

        @pl.when(is_owner)
        def _():
            await_bytes(r_zr.at[u, pl.ds(0, 7)], zr_rsem.at[u])
            for i in range(2):
                total = base[:, 128 * i : 128 * (i + 1)]
                for d in range(1, 8):
                    total = total + r_zr[u, lax.rem(z + d, 8), i].astype(F32)
                base[:, 128 * i : 128 * (i + 1)] = total

    def spread_send(u, pair):
        @pl.when(is_owner)
        def _():
            for i, part in enumerate(cut(pair)):
                r_d[u, i] = part.astype(BF)
            for d in (2, 1, 3):
                copy_out(r_d.at[u], r_d.at[u], d_ssem.at[u], d_rsem.at[u], {"row": row(d)})

    def spread_receive(u):
        @pl.when(is_owner)
        def _():
            for d in range(3):
                await_bytes(r_d.at[u], d_ssem.at[u])

        @pl.when(jnp.logical_not(is_owner))
        def _():
            await_bytes(r_d.at[u], d_rsem.at[u])

        return jnp.concatenate([r_d[u, 0], r_d[u, 1]], axis=1)

    def pack(parts, rows):
        return [jnp.concatenate([parts[2 * q][rows], parts[2 * q + 1][rows]], axis=0) for q in range(2)]

    def unpack(value):
        return jnp.concatenate([value[:8], value[8:]], axis=1)

    def from_reps(quarters):
        return jnp.concatenate(
            [jnp.concatenate([quarter[8 * k : 8 * k + 8] for quarter in quarters], axis=0) for k in range(2)],
            axis=1,
        )

    def out_send(place, value):
        for i in range(4):
            for k in range(2):
                s_out[place, i, k] = value[8 * i : 8 * (i + 1), 128 * k : 128 * (k + 1)]

        @pl.when(is_owner)
        def _():
            for d in range(8):
                n = lax.rem(lax.rem(c, 8) + d, 8)
                copy_out(
                    s_out.at[place, n // 2], r_out.at[place, lax.rem(z, 2)],
                    out_ssem.at[place], out_rsem.at[0],
                    {"col": 8 * h + n}, (c // 8 == h) if d == 0 else None,
                )

    def out_sent(place):
        @pl.when(is_owner)
        def _():
            await_bytes(s_out.at[place], out_ssem.at[place])
            await_bytes(s_out.at[place, pl.ds(0, 3)], out_ssem.at[place])

            @pl.when(c // 8 != h)
            def _():
                await_bytes(s_out.at[place, 3], out_ssem.at[place])

    def subtract(level, vectors, pair):
        acc[level] = acc[level] - contract(vectors, pair)

    loads["lui0"].wait()
    prepare_inverses(LUI, 1, lambda i, k: ls[k, i])
    loads["rhs"].wait()
    y0 = own_pair_inverse(jnp.concatenate([rhs[0, first_k], rhs[0, first_k + 1]], axis=1), LUI)
    y_keep[0] = y0
    for l in range(1, 5):
        acc[l] = rows_of(rhs, l, 0.125)
    loads["lu"].wait()
    mask_blocks(LU, 3, lambda i, k: lum[k, i])
    loads["lui"].wait()
    prepare_inverses(LUI + 1, 2, lambda i, k: ls[k, i + 1])
    turn_fold(0)
    barrier_wait()

    spread_send(0, y0)
    turn_send(0)
    for l in (1, 2):
        share(("lu", l), upper_pair(0, l), l)
    loads["lu later"].wait()
    mask_blocks(LU + 3, 7, lambda i, k: lum[k, i + 3])
    for l in (3, 4):
        share(("lu", l), upper_pair(0, l), l)
    loads["lui later"].wait()
    prepare_inverses(LUI + 3, 2, lambda i, k: ls[k, i + 3])
    for m in range(5):
        loads["cu", m].wait()
        mask_blocks(CU + 2 * m, 2, lambda i, k, m=m: cum[i, k, m])
    share("cu", CU, 10)
    loads["trhs"].wait()
    for a in range(2):
        acc[5 + a] = rows_of(trhs, a, 0.03125)
    shared["lu", 1].wait_recv()
    y0b = spread_receive(0)

    parts = apply_inverses(acc[1] - contract(y0b, upper_pair(0, 1)), LUI + 1)
    turn_relay(0)
    shared["lu", 2].wait_recv()
    gather_send(0, apply_inverses(acc[2] - contract(y0b, upper_pair(0, 2)), LUI + 2))
    z_send(0, parts)
    shared["lu", 3].wait_recv()
    shared["lu", 4].wait_recv()
    for l in (3, 4):
        subtract(l, y0b, upper_pair(0, l))
    shared["cu"].wait_recv()
    for a in range(2):
        subtract(5 + a, y0b, CU + a)
    turn_fold(1)
    turn_send(1)
    turn_share(0)
    gather_receive(0)
    turn_ready(0)
    y1 = z_receive(0, parts)

    pair = base[...] - contract_turned(y1.astype(BF), 0)
    x_send(0, pair)
    own = own_pair(y1)
    y_keep[1] = own
    spread_send(1, own)
    turn_relay(1)
    y1b = spread_receive(1)
    subtract(3, y1b, upper_pair(1, 3))
    subtract(4, y1b, upper_pair(1, 4))
    y2 = x_receive(0, pair)
    y_keep[2] = y2
    y2b = y2.astype(BF)

    parts = apply_inverses(acc[3] - contract(y2b, upper_pair(2, 3)), LUI + 3)
    gather_send(
        1,
        apply_inverses(
            acc[4] - contract(y2b, upper_pair(2, 4)), LUI + 4
        ),
    )
    z_send(1, parts)
    for a in range(2):
        acc[5 + a] = acc[5 + a] - contract(y1b, CU + 2 + a) - contract(y2b, CU + 4 + a)
    loads["tui"].wait()
    loads["tli"].wait()
    prepare_inverses(TUI, 1, lambda i, k: ts[i, k])
    prepare_inverses(TLI, 2, lambda i, k: ts[i, k])
    for k in range(4):
        upper = masked_inverse(TUI + 1, k, ts[1, k])
        keep_inverse(TUI + 1, k, times_inverse(upper, TLI + 1, k))
    turn_share(1)
    loads["lli"].wait()
    prepare_inverses(LLI, 5, lambda i, k: ls[k, i])
    loads["ll"].wait()
    mask_blocks(LL, 10, lambda i, k: llm[k, i])
    loads["tu"].wait()
    loads["tl"].wait()
    for u in (2, 3, 4):
        turn_fold(u)
        turn_send(u)
    gather_receive(1)
    turn_ready(1)
    y3 = z_receive(1, parts)

    pair = base[...] - contract_turned(y3.astype(BF), 1)
    x_send(1, pair)
    own = own_pair(y3)
    y_keep[3] = own
    spread_send(2, own)
    turn_relay(2)
    share("top", TU, 1)
    y3b = spread_receive(2)
    for a in range(2):
        subtract(5 + a, y3b, CU + 6 + a)
    y4 = x_receive(1, pair)
    y_keep[4] = y4
    y4b = y4.astype(BF)

    for a in range(2):
        parts = apply_inverses(acc[5 + a] - contract(y4b, CU + 8 + a), TUI + a)
        for rr in range(4):
            for q, packed in enumerate(pack(parts, slice(8 * rr, 8 * rr + 8))):
                s_cross[a, rr, q] = packed
        for e in (2, 1, 3):
            rr = lax.rem(r + e, 4)
            copy_out(
                s_cross.at[a, rr], r_cross.at[a, r], top_ssem.at[a], top_rsem.at[a], {"rep": rr}
            )
    for a in range(2):
        loads["cl", a].wait()
        mask_blocks(CL + 5 * a, 5, lambda i, k, a=a: clm[a, k, i])
    share("cl", CL, 10)

    def cross_receive(a):
        await_bytes(r_cross.at[a, pl.ds(0, 3)], top_ssem.at[a])
        await_bytes(r_cross.at[a, pl.ds(0, 3)], top_rsem.at[a])
        totals = []
        for q in range(2):
            total = s_cross[a, r, q]
            for e in range(1, 4):
                total = total + r_cross[a, lax.rem(r + e, 4), q]
            totals.append(total)
        return totals

    for q, packed in enumerate(cross_receive(0)):
        s_top0[q] = packed.astype(BF)
    for d in (2, 1, 3, 0):
        for q in range(2):
            copy_out(
                s_top0.at[q], r_top0.at[z], top_ssem.at[2], top_rsem.at[2],
                {"row": row(d), "col": 4 * x + 2 * q + h},
                (z == 2 * x + q) if d == 0 else None,
            )
    crossing = cross_receive(1)
    share("ll", LL, 10)
    turn_share(2)
    turn_ready(2)
    shared["top"].wait_recv()
    await_bytes(r_top0.at[pl.ds(0, 7)], top_ssem.at[2])

    @pl.when(jnp.logical_not(is_owner))
    def _():
        await_bytes(r_top0.at[7], top_ssem.at[2])

    await_bytes(r_top0, top_rsem.at[2])
    top0 = r_top0[0].astype(F32)
    for zz in range(1, 8):
        top0 = top0 + r_top0[zz].astype(F32)
    top0 = unpack(top0)

    parts = [-part for part in apply_inverses(contract(top0.astype(BF), TU), TUI + 1)]
    mine = [crossing[q] + packed for q, packed in enumerate(pack(parts, slice(0, 8)))]
    for q in range(2):
        s_mid[q] = mine[q].astype(BF)
    for d in (4, 3, 5, 2, 6, 1, 7):
        copy_out(s_mid, r_mid.at[z], top_ssem.at[3], top_rsem.at[3], {"col": chip(d)})
    top0_base = own_pair_inverse(top0, TLI) * owner
    await_bytes(r_mid.at[pl.ds(0, 7)], top_ssem.at[3])
    await_bytes(r_mid.at[pl.ds(0, 7)], top_rsem.at[3])
    for q in range(2):
        for d in range(1, 8):
            mine[q] = mine[q] + r_mid[lax.rem(z + d, 8), q].astype(F32)

    vectors = jnp.concatenate([unpack(mine[q]) for q in range(2)], axis=1).astype(BF)
    pair = top0_base - contract_turned(vectors, 2)
    here = 4 * r + x
    r_low[here] = jnp.concatenate(cut(pair), axis=0)
    for e in (2, 1, 3, 0):
        for d in (2, 1, 3, 0):
            if d or e:
                copy_out(
                    r_low.at[here], r_low.at[here], top_ssem.at[4], top_rsem.at[4],
                    {"row": row(d), "rep": lax.rem(r + e, 4)},
                )

    @pl.when(is_owner)
    def _():
        xt1[r] = jnp.where(even, mine[0], mine[1])
        for e in (2, 1, 3, 0):
            for d in (2, 1, 3, 0):
                if d or e:
                    copy_out(
                        xt1.at[r], xt1.at[r], top_ssem.at[6], top_rsem.at[6],
                        {"row": row(d), "rep": lax.rem(r + e, 4)},
                    )

    turn_relay(3)
    for l in range(5):
        acc[l] = owned(y_keep[l])
    @pl.when(is_owner)
    def _():
        for _ in range(5):
            await_bytes(xt1.at[pl.ds(0, 3)], top_ssem.at[6])
        await_bytes(xt1.at[pl.ds(0, 3)], top_rsem.at[6])

    @pl.when(jnp.logical_not(is_owner))
    def _():
        await_bytes(xt1, top_rsem.at[6])

    x_top1 = from_reps([xt1[rr] for rr in range(4)])
    xt1b = x_top1.astype(BF)
    shared["cl"].wait_recv()
    subtract(4, xt1b, CL + 9)
    subtract(3, xt1b, CL + 8)
    await_bytes(r_low.at[pl.ds(0, 15)], top_ssem.at[4])
    await_bytes(r_low.at[pl.ds(0, 15)], top_rsem.at[4])
    x_top0 = from_reps([sum(r_low[4 * rr + xx] for xx in range(4)) for rr in range(4)])
    xt0b = x_top0.astype(BF)

    parts = apply_inverses(acc[4] - contract(xt0b, CL + 4), LLI + 4)
    gather_send(
        2, apply_inverses(acc[3] - contract(xt0b, CL + 3), LLI + 3)
    )
    z_send(2, parts)
    out_send(5, x_top1)
    out_send(4, x_top0)
    for l in (2, 1, 0):
        acc[l] = acc[l] - contract(xt1b, CL + 5 + l) - contract(xt0b, CL + l)
    turn_share(3)
    gather_receive(2)
    turn_ready(3)
    x4 = z_receive(2, parts)

    pair = base[...] - contract_turned(x4.astype(BF), 3)
    x_send(2, pair)
    own = own_pair(x4)
    spread_send(3, own)
    turn_relay(4)
    out_send(3, own)
    shared["ll"].wait_recv()
    x4b = spread_receive(3)
    subtract(2, x4b, lower_pair(2, 4))
    subtract(1, x4b, lower_pair(1, 4))
    x3 = x_receive(2, pair)
    x3b = x3.astype(BF)

    parts = apply_inverses(acc[2] - contract(x3b, lower_pair(2, 3)), LLI + 2)
    gather_send(
        3,
        apply_inverses(
            acc[1] - contract(x3b, lower_pair(1, 3)), LLI + 1
        ),
    )
    z_send(3, parts)
    out_send(2, x3)
    acc[0] = acc[0] - contract(x4b, lower_pair(0, 4)) - contract(x3b, lower_pair(0, 3))
    turn_share(4)
    gather_receive(3)
    turn_ready(4)
    x2 = z_receive(3, parts)

    pair = base[...] - contract_turned(x2.astype(BF), 4)
    x_send(3, pair)
    own = own_pair(x2)
    spread_send(4, own)
    out_send(1, own)
    x2b = spread_receive(4)
    subtract(0, x2b, lower_pair(0, 2))
    x1 = x_receive(3, pair)
    x1b = x1.astype(BF)

    parts = apply_inverses(acc[0] - contract(x1b, lower_pair(0, 1)), LLI)
    for i in range(4):
        for q, packed in enumerate(pack(parts, slice(8 * i, 8 * i + 8))):
            s_last[i, q] = packed.astype(BF)
    for d in (4, 3, 5, 2, 6, 1, 7, 0):
        n = lax.rem(lax.rem(c, 8) + d, 8)
        copy_out(
            s_last.at[n // 2], r_last.at[z], top_ssem.at[7], top_rsem.at[7],
            {"col": 8 * h + n}, (c // 8 == h) if d == 0 else None,
        )
    out_send(0, x1)

    def own_rows(value):
        return jnp.where(h == 0, value[0:4], value[4:8])

    for copy in shared.values():
        copy.wait_send()
    for place in range(6):
        out_sent(place)
    await_bytes(r_last.at[pl.ds(0, 7)], top_ssem.at[7])

    @pl.when(h != c // 8)
    def _():
        await_bytes(r_last.at[7], top_ssem.at[7])

    await_bytes(r_out, out_rsem.at[0])
    for place in range(6):
        for k in range(4):
            value = own_rows(r_out[place, k // 2, k % 2])
            if place == 5:
                out[6, k] = value
            elif place == 4:
                out[5, k] = value
            else:
                out[place + 1, k] = value
    await_bytes(r_last, top_rsem.at[7])
    for q in range(2):
        last = r_last[0, q].astype(F32)
        for zz in range(1, 8):
            last = last + r_last[zz, q].astype(F32)
        for i in range(2):
            out[0, 2 * q + i] = own_rows(last[8 * i : 8 * i + 8])


def on_device(
    right_side, top_right_side, leaf_upper, leaf_upper_mask, leaf_lower, leaf_lower_mask, cross_upper, cross_upper_mask,
    cross_lower, cross_lower_mask, top_upper, top_lower, leaf_upper_inverse, leaf_lower_inverse, top_upper_inverse,
    top_lower_inverse, leaf_sizes, top_sizes,
):
    in_hbm = pl.BlockSpec(memory_space=pl.ANY)
    in_smem = pl.BlockSpec(memory_space=pltpu.SMEM)
    in_vmem = pl.BlockSpec(memory_space=pltpu.VMEM)
    dma = pltpu.SemaphoreType.DMA
    out = pl.pallas_call(
        kernel,
        out_shape=jax.ShapeDtypeStruct((7, 4, 4, 128), F32),
        in_specs=[in_hbm] * 12 + [in_smem] * 6,
        out_specs=in_vmem,
        scratch_shapes=[
            pltpu.VMEM((42, 2, 4, 128, 128), BF),
            pltpu.VMEM((14, 4, 128, 128), F32),
            pltpu.VMEM((14, 4, 128, 256), BF),
            pltpu.VMEM((5, 4, 32, 128), F32),
            pltpu.VMEM((2, 4, 32, 128), F32),
            pltpu.VMEM((7, 32, 512), F32),
            pltpu.VMEM((5, 32, 256), F32),
            pltpu.VMEM((32, 256), F32),
            pltpu.VMEM((5, 4, 128, 128), BF),
            pltpu.VMEM((5, 4, 128, 128), BF),
            pltpu.VMEM((5, 4, 2, 128, 128), BF),
            pltpu.VMEM((4, 4, 32, 128), BF),
            pltpu.VMEM((4, 8, 4, 32, 128), BF),
            pltpu.VMEM((4, 2, 32, 128), BF),
            pltpu.VMEM((4, 4, 2, 32, 128), BF),
            pltpu.VMEM((4, 2, 2, 32, 128), BF),
            pltpu.VMEM((4, 8, 2, 32, 128), BF),
            pltpu.VMEM((5, 2, 32, 128), BF),
            pltpu.VMEM((2, 4, 2, 16, 128), F32),
            pltpu.VMEM((2, 4, 2, 16, 128), F32),
            pltpu.VMEM((2, 16, 128), BF),
            pltpu.VMEM((8, 16, 128), BF),
            pltpu.VMEM((2, 16, 128), BF),
            pltpu.VMEM((8, 2, 16, 128), BF),
            pltpu.VMEM((16, 16, 128), F32),
            pltpu.VMEM((4, 16, 128), F32),
            pltpu.VMEM((4, 2, 16, 128), BF),
            pltpu.VMEM((8, 2, 16, 128), BF),
            pltpu.VMEM((6, 4, 2, 8, 128), F32),
            pltpu.VMEM((6, 2, 2, 8, 128), F32),
        ]
        + [dma((n,)) for n in (20, 8, 8, 4, 4, 4, 4, 4, 4, 5, 5, 5, 5, 5, 5, 5, 5, 8, 8, 6, 1)],
        compiler_params=pltpu.CompilerParams(
            collective_id=0, has_side_effects=True, vmem_limit_bytes=58 * 1024 * 1024
        ),
    )(
        right_side, top_right_side, leaf_upper, leaf_lower, cross_upper, cross_lower, top_upper, top_lower,
        leaf_upper_inverse, leaf_lower_inverse, top_upper_inverse, top_lower_inverse,
        leaf_upper_mask[0, :, 0].T, leaf_lower_mask[0, :, 0].T,
        cross_upper_mask[0, :, 0].transpose(1, 2, 0), cross_lower_mask[0, :, 0].transpose(0, 2, 1),
        leaf_sizes[0].T, top_sizes,
    )
    return out[None, :5], out[5:]


def solution(mesh):
    in_specs = (
        P("rep", None, "row", None, None),
        P(None, "row", None, None),
        P("rep", None, "col", "row", None, None),
        P("rep", None, "col", "row"),
        P("rep", None, "col", "row", None, None),
        P("rep", None, "col", "row"),
        P("rep", None, "col", None, "row", None, None),
        P("rep", None, "col", None, "row"),
        P("rep", None, "col", None, "row", None, None),
        P("rep", None, "col", None, "row"),
        P(None, "col", "row", None, None),
        P(None, "col", "row", None, None),
        P("rep", None, "row", None, None),
        P("rep", None, "row", None, None),
        P(None, "row", None, None),
        P(None, "row", None, None),
        P("rep", None, "row"),
        P(None, "row"),
    )
    out_specs = (P("rep", None, "row", "col", None), P(None, "row", "col", None))
    return jax.shard_map(
        on_device, mesh=mesh, in_specs=in_specs, out_specs=out_specs, check_vma=False
    )
```

```python
import jax
import jax.numpy as jnp
from jax import lax
from jax.experimental import pallas as pl
from jax.experimental.pallas import tpu as pltpu
from jax.sharding import PartitionSpec as P

MESH = pl.DeviceIdType.MESH
BF = jnp.bfloat16
F32 = jnp.float32

LU, CU, CL, LL, TU, TL = 0, 10, 20, 30, 40, 41
LUI, LLI, TUI, TLI = 0, 5, 10, 12


def upper_pair(m, l):
    return LU + l * (l - 1) // 2 + m


def lower_pair(l, m):
    q = 4 - l
    return LL + q * (q - 1) // 2 + (m - l - 1)


TURNED = (
    (upper_pair(1, 2), LUI + 2),
    (upper_pair(3, 4), LUI + 4),
    (TL, TLI),
    (lower_pair(3, 4), LLI + 3),
    (lower_pair(1, 2), LLI + 1),
)


def kernel(
    rs, trs, lu, ll, cu, cl, tu, tl, lui, lli, tui, tli,
    lum, llm, cum, clm, ls, ts,
    out,
    blk, inv_raw, inv, rhs, trhs, acc, y_keep, base,
    turn_out, relay, turn,
    s_z, r_z, s_x, r_x, s_zr, r_zr, r_d,
    s_cross, r_cross, s_top0, r_top0, s_mid, r_mid, r_low, xt1,
    s_last, r_last, s_out, r_out,
    load_sem, pair_ssem, pair_rsem, z_ssem, z_rsem, x_ssem, x_rsem, zr_ssem, zr_rsem, d_ssem, d_rsem,
    v_ssem, v_rsem, t_ssem, t_rsem, ts_ssem, ts_rsem, top_ssem, top_rsem, out_ssem, out_rsem,
):
    x = lax.axis_index("row")
    c = lax.axis_index("col")
    r = lax.axis_index("rep")
    z, h = c // 2, lax.rem(c, 2)
    even = lax.rem(z, 2) == 0
    first_k = 2 * lax.rem(z, 2)
    sibling = {"col": c + 1 - 2 * h}
    is_owner = (z // 2) == x
    owner = jnp.where(is_owner, 1.0, 0.0).astype(F32)
    low = jnp.where(z == 2 * x, 1.0, 0.0).astype(F32)
    high = jnp.where(z == 2 * x + 1, 1.0, 0.0).astype(F32)

    def row(d):
        return lax.rem(x + d, 4)

    def chip(d):
        return 2 * lax.rem(z + d, 8) + h

    half = pl.ds(pl.multiple_of(32 * h, 32), 32)
    loads = {}

    def load(name, src, dst):
        copy = pltpu.make_async_copy(src, dst, load_sem.at[len(loads)])
        copy.start()
        loads[name] = copy

    load("lui0", lui.at[0, pl.ds(0, 1)], inv_raw.at[pl.ds(LUI, 1)])
    load("rhs", rs.at[0, :, :, half], rhs)
    load("lu", lu.at[0, pl.ds(0, 3), 0], blk.at[pl.ds(LU, 3), h])
    load("lui", lui.at[0, pl.ds(1, 2)], inv_raw.at[pl.ds(LUI + 1, 2)])
    load("lu later", lu.at[0, pl.ds(3, 7), 0], blk.at[pl.ds(LU + 3, 7), h])
    load("lui later", lui.at[0, pl.ds(3, 2)], inv_raw.at[pl.ds(LUI + 3, 2)])
    for m in range(5):
        load(("cu", m), cu.at[0, m, 0], blk.at[pl.ds(CU + 2 * m, 2), h])
    load("trhs", trs.at[:, :, half], trhs)
    load("tui", tui, inv_raw.at[pl.ds(TUI, 2)])
    load("tli", tli, inv_raw.at[pl.ds(TLI, 2)])
    load("tu", tu.at[0], blk.at[pl.ds(TU, 1), h])
    load("tl", tl.at[0], blk.at[pl.ds(TL, 1), h])
    for a in range(2):
        load(("cl", a), cl.at[0, a, 0], blk.at[pl.ds(CL + 5 * a, 5), h])
    load("lli", lli.at[0], inv_raw.at[pl.ds(LLI, 5)])
    load("ll", ll.at[0, :, 0], blk.at[pl.ds(LL, 10), h])

    barrier = pltpu.get_barrier_semaphore()

    def greet(device):
        pl.semaphore_signal(barrier, inc=1, device_id=device, device_id_type=MESH)

    for d in (4, 3, 5, 2, 6, 1, 7):
        greet({"col": chip(d)})
    for d in (2, 1, 3):
        greet({"row": row(d)})
        greet({"rep": lax.rem(r + d, 4)})
    greet(sibling)

    def barrier_wait():
        pl.semaphore_wait(barrier, 14)

    def split(value):
        hi = value.astype(BF)
        return hi, (value - hi.astype(F32)).astype(BF)

    def masked_inverse(place, k, size):
        value = inv_raw[place, k]
        down = lax.broadcasted_iota(jnp.int32, (128, 128), 0)
        across = lax.broadcasted_iota(jnp.int32, (128, 128), 1)
        return jnp.where(jnp.maximum(down, across) < size, value, 0.0)

    def keep_inverse(place, k, value):
        hi, lo = split(value)
        inv[place, k, :, 0:128] = hi
        inv[place, k, :, 128:256] = lo

    def prepare_inverses(first, count, size_of):
        for i in range(count):
            for k in range(4):
                keep_inverse(first + i, k, masked_inverse(first + i, k, size_of(i, k)))

    def times_inverse(value, place, k):
        rows = value.shape[0]
        hi, lo = split(value)
        both = jnp.concatenate([hi, lo], axis=0)
        wide = jnp.dot(both, inv[place, k], preferred_element_type=F32)
        return wide[:rows, :128] + wide[rows:, :128] + wide[:rows, 128:]

    def cut(value):
        return [value[:, 128 * k : 128 * (k + 1)] for k in range(value.shape[1] // 128)]

    def apply_inverses(value, place):
        return [times_inverse(part, place, k) for k, part in enumerate(cut(value))]

    def own_pair_inverse(pair, place):
        return jnp.concatenate(
            [times_inverse(part, place, first_k + i) for i, part in enumerate(cut(pair))], axis=1
        )

    def contract(vectors, pair):
        columns = [
            jnp.concatenate([blk[pair, 0, k], blk[pair, 1, k]], axis=0) for k in range(4)
        ]
        return jnp.dot(vectors, jnp.concatenate(columns, axis=1), preferred_element_type=F32)

    def contract_turned(vectors, u):
        columns = [
            jnp.concatenate([turn[u, j, i] for j in range(4)], axis=0) for i in range(2)
        ]
        return jnp.dot(vectors, jnp.concatenate(columns, axis=1), preferred_element_type=F32)

    def mask_blocks(first, count, flag_of):
        def body(i, _):
            for k in range(4):
                flag = jnp.full((128, 128), flag_of(i, k).astype(F32), F32).astype(BF)
                blk[first + i, h, k] = blk[first + i, h, k] * flag
            return 0

        lax.fori_loop(0, count, body, 0)

    def remote_copy(src, dst, ssem, rsem, device):
        return pltpu.make_async_remote_copy(
            src_ref=src, dst_ref=dst, send_sem=ssem, recv_sem=rsem, device_id=device, device_id_type=MESH
        )

    def copy_out(src, dst, ssem, rsem, device, is_self=None):
        remote = remote_copy(src, dst, ssem, rsem, device)
        if is_self is None:
            remote.start()
            return

        @pl.when(is_self)
        def _():
            pltpu.make_async_copy(src, dst, rsem).start()

        @pl.when(jnp.logical_not(is_self))
        def _():
            remote.start()

    def await_bytes(ref, sem):
        pltpu.make_async_copy(ref, ref, sem).wait()

    shared = {}

    def share(name, first, count):
        at = len(shared)
        part = blk.at[pl.ds(first, count), h]
        copy = remote_copy(part, part, pair_ssem.at[at], pair_rsem.at[at], sibling)
        copy.start()
        shared[name] = copy

    def rows_of(source, level, scale):
        return jnp.concatenate([source[level, k] * scale for k in range(4)], axis=1)

    def owned(pair):
        return jnp.concatenate([pair * low, pair * high], axis=1)

    def own_pair(value):
        return jnp.where(even, value[:, :256], value[:, 256:])

    def turn_fold(u):
        pair, place = TURNED[u]
        for k in range(4):
            wide = jnp.dot(blk[pair, h, k], inv[place, k], preferred_element_type=F32)
            turn_out[u, k] = (wide[:, :128] + wide[:, 128:]).astype(BF)

    def turn_send(u):
        for d in (2, 1, 3):
            copy_out(turn_out.at[u, d], relay.at[u, x], v_ssem.at[u], v_rsem.at[u], {"row": row(d)})
        relay[u, x] = turn_out[u, 0]

    def turn_relay(u):
        await_bytes(relay.at[u, pl.ds(0, 3)], v_ssem.at[u])
        await_bytes(relay.at[u, pl.ds(0, 3)], v_rsem.at[u])
        for d in range(4):
            source = row(d)
            k = (4 - d) % 4
            copy_out(
                relay.at[u, source], turn.at[u, lax.rem(c, 4), k % 2], t_ssem.at[u], t_rsem.at[u],
                {"row": c // 4, "col": 4 * source + 2 * (k // 2) + h},
                (z == 2 * x) if d == 0 else None,
            )

    def turn_share(u):
        await_bytes(turn.at[u, pl.ds(0, 2)], t_rsem.at[u])
        await_bytes(relay.at[u, pl.ds(0, 3)], t_ssem.at[u])

        @pl.when(z != 2 * x)
        def _():
            await_bytes(relay.at[u, 3], t_ssem.at[u])

        for j in range(2):
            part = turn.at[u, 2 * j + h]
            remote_copy(part, part, ts_ssem.at[u], ts_rsem.at[u], sibling).start()

    def turn_ready(u):
        await_bytes(turn.at[u, pl.ds(0, 2)], ts_ssem.at[u])
        await_bytes(turn.at[u, pl.ds(0, 2)], ts_rsem.at[u])

    def z_send(step, parts):
        for k in range(4):
            s_z[step, k] = parts[k].astype(BF)
        for d in (4, 3, 5, 2, 6, 1, 7):
            copy_out(s_z.at[step], r_z.at[step, z], z_ssem.at[step], z_rsem.at[step], {"col": chip(d)})

    def z_receive(step, parts):
        await_bytes(r_z.at[step, pl.ds(0, 7)], z_ssem.at[step])
        await_bytes(r_z.at[step, pl.ds(0, 7)], z_rsem.at[step])
        totals = []
        for k in range(4):
            total = parts[k]
            for d in range(1, 8):
                total = total + r_z[step, lax.rem(z + d, 8), k].astype(F32)
            totals.append(total)
        return jnp.concatenate(totals, axis=1)

    def x_send(step, pair):
        for i, part in enumerate(cut(pair)):
            s_x[step, i] = part.astype(BF)
        for d in (2, 1, 3):
            copy_out(s_x.at[step], r_x.at[step, x], x_ssem.at[step], x_rsem.at[step], {"row": row(d)})

    def x_receive(step, pair):
        await_bytes(r_x.at[step, pl.ds(0, 3)], x_ssem.at[step])
        await_bytes(r_x.at[step, pl.ds(0, 3)], x_rsem.at[step])
        totals = []
        for i, total in enumerate(cut(pair)):
            for d in range(1, 4):
                total = total + r_x[step, row(d), i].astype(F32)
            totals.append(total)
        return jnp.concatenate(totals, axis=1)

    def gather_send(u, parts):
        for k in range(4):
            s_zr[u, k // 2, k % 2] = parts[k].astype(BF)
        for q in range(2):
            @pl.when(z != 2 * x + q)
            def _(q=q):
                copy_out(
                    s_zr.at[u, q], r_zr.at[u, z], zr_ssem.at[u], zr_rsem.at[u], {"col": 4 * x + 2 * q + h}
                )
        base[...] = own_pair(jnp.concatenate(parts, axis=1))

    def gather_receive(u):
        await_bytes(s_zr.at[u, 0], zr_ssem.at[u])

        @pl.when(jnp.logical_not(is_owner))
        def _():
            await_bytes(s_zr.at[u, 1], zr_ssem.at[u])
            base[...] = jnp.zeros_like(base)

        @pl.when(is_owner)
        def _():
            await_bytes(r_zr.at[u, pl.ds(0, 7)], zr_rsem.at[u])
            for i in range(2):
                total = base[:, 128 * i : 128 * (i + 1)]
                for d in range(1, 8):
                    total = total + r_zr[u, lax.rem(z + d, 8), i].astype(F32)
                base[:, 128 * i : 128 * (i + 1)] = total

    def spread_send(u, pair):
        @pl.when(is_owner)
        def _():
            for i, part in enumerate(cut(pair)):
                r_d[u, i] = part.astype(BF)
            for d in (2, 1, 3):
                copy_out(r_d.at[u], r_d.at[u], d_ssem.at[u], d_rsem.at[u], {"row": row(d)})

    def spread_receive(u):
        @pl.when(is_owner)
        def _():
            for d in range(3):
                await_bytes(r_d.at[u], d_ssem.at[u])

        @pl.when(jnp.logical_not(is_owner))
        def _():
            await_bytes(r_d.at[u], d_rsem.at[u])

        return jnp.concatenate([r_d[u, 0], r_d[u, 1]], axis=1)

    def pack(parts, rows):
        return [jnp.concatenate([parts[2 * q][rows], parts[2 * q + 1][rows]], axis=0) for q in range(2)]

    def unpack(value):
        return jnp.concatenate([value[:8], value[8:]], axis=1)

    def from_reps(quarters):
        return jnp.concatenate(
            [jnp.concatenate([quarter[8 * k : 8 * k + 8] for quarter in quarters], axis=0) for k in range(2)],
            axis=1,
        )

    def out_send(place, value):
        for i in range(4):
            for k in range(2):
                s_out[place, i, k] = value[8 * i : 8 * (i + 1), 128 * k : 128 * (k + 1)]

        @pl.when(is_owner)
        def _():
            for d in range(8):
                n = lax.rem(lax.rem(c, 8) + d, 8)
                copy_out(
                    s_out.at[place, n // 2], r_out.at[place, lax.rem(z, 2)],
                    out_ssem.at[place], out_rsem.at[0],
                    {"col": 8 * h + n}, (c // 8 == h) if d == 0 else None,
                )

    def out_sent(place):
        @pl.when(is_owner)
        def _():
            await_bytes(s_out.at[place], out_ssem.at[place])
            await_bytes(s_out.at[place, pl.ds(0, 3)], out_ssem.at[place])

            @pl.when(c // 8 != h)
            def _():
                await_bytes(s_out.at[place, 3], out_ssem.at[place])

    def subtract(level, vectors, pair):
        acc[level] = acc[level] - contract(vectors, pair)

    loads["lui0"].wait()
    prepare_inverses(LUI, 1, lambda i, k: ls[k, i])
    loads["rhs"].wait()
    y0 = own_pair_inverse(jnp.concatenate([rhs[0, first_k], rhs[0, first_k + 1]], axis=1), LUI)
    y_keep[0] = y0
    for l in range(1, 5):
        acc[l] = rows_of(rhs, l, 0.125)
    loads["lu"].wait()
    mask_blocks(LU, 3, lambda i, k: lum[k, i])
    loads["lui"].wait()
    prepare_inverses(LUI + 1, 2, lambda i, k: ls[k, i + 1])
    turn_fold(0)
    barrier_wait()

    spread_send(0, y0)
    turn_send(0)
    for l in (1, 2):
        share(("lu", l), upper_pair(0, l), l)
    loads["lu later"].wait()
    mask_blocks(LU + 3, 7, lambda i, k: lum[k, i + 3])
    for l in (3, 4):
        share(("lu", l), upper_pair(0, l), l)
    loads["lui later"].wait()
    prepare_inverses(LUI + 3, 2, lambda i, k: ls[k, i + 3])
    for m in range(5):
        loads["cu", m].wait()
        mask_blocks(CU + 2 * m, 2, lambda i, k, m=m: cum[i, k, m])
    share("cu", CU, 10)
    loads["trhs"].wait()
    for a in range(2):
        acc[5 + a] = rows_of(trhs, a, 0.03125)
    shared["lu", 1].wait_recv()
    y0b = spread_receive(0)

    parts = apply_inverses(acc[1] - contract(y0b, upper_pair(0, 1)), LUI + 1)
    turn_relay(0)
    shared["lu", 2].wait_recv()
    gather_send(0, apply_inverses(acc[2] - contract(y0b, upper_pair(0, 2)), LUI + 2))
    z_send(0, parts)
    shared["lu", 3].wait_recv()
    shared["lu", 4].wait_recv()
    for l in (3, 4):
        subtract(l, y0b, upper_pair(0, l))
    shared["cu"].wait_recv()
    for a in range(2):
        subtract(5 + a, y0b, CU + a)
    turn_share(0)
    turn_fold(1)
    turn_send(1)
    gather_receive(0)
    turn_ready(0)
    y1 = z_receive(0, parts)

    pair = base[...] - contract_turned(y1.astype(BF), 0)
    x_send(0, pair)
    own = own_pair(y1)
    y_keep[1] = own
    spread_send(1, own)
    turn_relay(1)
    y1b = spread_receive(1)
    subtract(3, y1b, upper_pair(1, 3))
    subtract(4, y1b, upper_pair(1, 4))
    y2 = x_receive(0, pair)
    y_keep[2] = y2
    y2b = y2.astype(BF)

    parts = apply_inverses(acc[3] - contract(y2b, upper_pair(2, 3)), LUI + 3)
    gather_send(
        1,
        apply_inverses(
            acc[4] - contract(y2b, upper_pair(2, 4)), LUI + 4
        ),
    )
    z_send(1, parts)
    for a in range(2):
        acc[5 + a] = acc[5 + a] - contract(y1b, CU + 2 + a) - contract(y2b, CU + 4 + a)
    loads["tui"].wait()
    loads["tli"].wait()
    prepare_inverses(TUI, 1, lambda i, k: ts[i, k])
    prepare_inverses(TLI, 2, lambda i, k: ts[i, k])
    for k in range(4):
        upper = masked_inverse(TUI + 1, k, ts[1, k])
        keep_inverse(TUI + 1, k, times_inverse(upper, TLI + 1, k))
    turn_share(1)
    loads["lli"].wait()
    prepare_inverses(LLI, 5, lambda i, k: ls[k, i])
    loads["ll"].wait()
    mask_blocks(LL, 10, lambda i, k: llm[k, i])
    loads["tu"].wait()
    loads["tl"].wait()
    for u in (2, 3, 4):
        turn_fold(u)
        turn_send(u)
    gather_receive(1)
    turn_ready(1)
    y3 = z_receive(1, parts)

    pair = base[...] - contract_turned(y3.astype(BF), 1)
    x_send(1, pair)
    own = own_pair(y3)
    y_keep[3] = own
    spread_send(2, own)
    turn_relay(2)
    share("top", TU, 1)
    y3b = spread_receive(2)
    for a in range(2):
        subtract(5 + a, y3b, CU + 6 + a)
    y4 = x_receive(1, pair)
    y_keep[4] = y4
    y4b = y4.astype(BF)

    for a in range(2):
        parts = apply_inverses(acc[5 + a] - contract(y4b, CU + 8 + a), TUI + a)
        for rr in range(4):
            for q, packed in enumerate(pack(parts, slice(8 * rr, 8 * rr + 8))):
                s_cross[a, rr, q] = packed
        for e in (2, 1, 3):
            rr = lax.rem(r + e, 4)
            copy_out(
                s_cross.at[a, rr], r_cross.at[a, r], top_ssem.at[a], top_rsem.at[a], {"rep": rr}
            )
    for a in range(2):
        loads["cl", a].wait()
        mask_blocks(CL + 5 * a, 5, lambda i, k, a=a: clm[a, k, i])
    share("cl", CL, 10)

    def cross_receive(a):
        await_bytes(r_cross.at[a, pl.ds(0, 3)], top_ssem.at[a])
        await_bytes(r_cross.at[a, pl.ds(0, 3)], top_rsem.at[a])
        totals = []
        for q in range(2):
            total = s_cross[a, r, q]
            for e in range(1, 4):
                total = total + r_cross[a, lax.rem(r + e, 4), q]
            totals.append(total)
        return totals

    for q, packed in enumerate(cross_receive(0)):
        s_top0[q] = packed.astype(BF)
    for d in (2, 1, 3, 0):
        for q in range(2):
            copy_out(
                s_top0.at[q], r_top0.at[z], top_ssem.at[2], top_rsem.at[2],
                {"row": row(d), "col": 4 * x + 2 * q + h},
                (z == 2 * x + q) if d == 0 else None,
            )
    crossing = cross_receive(1)
    share("ll", LL, 10)
    turn_share(2)
    turn_ready(2)
    shared["top"].wait_recv()
    await_bytes(r_top0.at[pl.ds(0, 7)], top_ssem.at[2])

    @pl.when(jnp.logical_not(is_owner))
    def _():
        await_bytes(r_top0.at[7], top_ssem.at[2])

    await_bytes(r_top0, top_rsem.at[2])
    top0 = r_top0[0].astype(F32)
    for zz in range(1, 8):
        top0 = top0 + r_top0[zz].astype(F32)
    top0 = unpack(top0)

    parts = [-part for part in apply_inverses(contract(top0.astype(BF), TU), TUI + 1)]
    mine = [crossing[q] + packed for q, packed in enumerate(pack(parts, slice(0, 8)))]
    for q in range(2):
        s_mid[q] = mine[q].astype(BF)
    for d in (4, 3, 5, 2, 6, 1, 7):
        copy_out(s_mid, r_mid.at[z], top_ssem.at[3], top_rsem.at[3], {"col": chip(d)})
    top0_base = own_pair_inverse(top0, TLI) * owner
    await_bytes(r_mid.at[pl.ds(0, 7)], top_ssem.at[3])
    await_bytes(r_mid.at[pl.ds(0, 7)], top_rsem.at[3])
    for q in range(2):
        for d in range(1, 8):
            mine[q] = mine[q] + r_mid[lax.rem(z + d, 8), q].astype(F32)

    vectors = jnp.concatenate([unpack(mine[q]) for q in range(2)], axis=1).astype(BF)
    pair = top0_base - contract_turned(vectors, 2)
    here = 4 * r + x
    r_low[here] = jnp.concatenate(cut(pair), axis=0)
    for e in (2, 1, 3, 0):
        for d in (2, 1, 3, 0):
            if d or e:
                copy_out(
                    r_low.at[here], r_low.at[here], top_ssem.at[4], top_rsem.at[4],
                    {"row": row(d), "rep": lax.rem(r + e, 4)},
                )

    @pl.when(is_owner)
    def _():
        xt1[r] = jnp.where(even, mine[0], mine[1])
        for e in (2, 1, 3, 0):
            for d in (2, 1, 3, 0):
                if d or e:
                    copy_out(
                        xt1.at[r], xt1.at[r], top_ssem.at[6], top_rsem.at[6],
                        {"row": row(d), "rep": lax.rem(r + e, 4)},
                    )

    turn_relay(3)
    for l in range(5):
        acc[l] = owned(y_keep[l])
    @pl.when(is_owner)
    def _():
        for _ in range(5):
            await_bytes(xt1.at[pl.ds(0, 3)], top_ssem.at[6])
        await_bytes(xt1.at[pl.ds(0, 3)], top_rsem.at[6])

    @pl.when(jnp.logical_not(is_owner))
    def _():
        await_bytes(xt1, top_rsem.at[6])

    x_top1 = from_reps([xt1[rr] for rr in range(4)])
    xt1b = x_top1.astype(BF)
    shared["cl"].wait_recv()
    subtract(4, xt1b, CL + 9)
    subtract(3, xt1b, CL + 8)
    await_bytes(r_low.at[pl.ds(0, 15)], top_ssem.at[4])
    await_bytes(r_low.at[pl.ds(0, 15)], top_rsem.at[4])
    x_top0 = from_reps([sum(r_low[4 * rr + xx] for xx in range(4)) for rr in range(4)])
    xt0b = x_top0.astype(BF)

    parts = apply_inverses(acc[4] - contract(xt0b, CL + 4), LLI + 4)
    gather_send(
        2, apply_inverses(acc[3] - contract(xt0b, CL + 3), LLI + 3)
    )
    z_send(2, parts)
    out_send(5, x_top1)
    out_send(4, x_top0)
    for l in (2, 1, 0):
        acc[l] = acc[l] - contract(xt1b, CL + 5 + l) - contract(xt0b, CL + l)
    turn_share(3)
    gather_receive(2)
    turn_ready(3)
    x4 = z_receive(2, parts)

    pair = base[...] - contract_turned(x4.astype(BF), 3)
    x_send(2, pair)
    own = own_pair(x4)
    spread_send(3, own)
    turn_relay(4)
    out_send(3, own)
    shared["ll"].wait_recv()
    x4b = spread_receive(3)
    subtract(2, x4b, lower_pair(2, 4))
    subtract(1, x4b, lower_pair(1, 4))
    x3 = x_receive(2, pair)
    x3b = x3.astype(BF)

    parts = apply_inverses(acc[2] - contract(x3b, lower_pair(2, 3)), LLI + 2)
    gather_send(
        3,
        apply_inverses(
            acc[1] - contract(x3b, lower_pair(1, 3)), LLI + 1
        ),
    )
    z_send(3, parts)
    out_send(2, x3)
    acc[0] = acc[0] - contract(x4b, lower_pair(0, 4)) - contract(x3b, lower_pair(0, 3))
    turn_share(4)
    gather_receive(3)
    turn_ready(4)
    x2 = z_receive(3, parts)

    pair = base[...] - contract_turned(x2.astype(BF), 4)
    x_send(3, pair)
    own = own_pair(x2)
    spread_send(4, own)
    out_send(1, own)
    x2b = spread_receive(4)
    subtract(0, x2b, lower_pair(0, 2))
    x1 = x_receive(3, pair)
    x1b = x1.astype(BF)

    parts = apply_inverses(acc[0] - contract(x1b, lower_pair(0, 1)), LLI)
    for i in range(4):
        for q, packed in enumerate(pack(parts, slice(8 * i, 8 * i + 8))):
            s_last[i, q] = packed.astype(BF)
    for d in (4, 3, 5, 2, 6, 1, 7, 0):
        n = lax.rem(lax.rem(c, 8) + d, 8)
        copy_out(
            s_last.at[n // 2], r_last.at[z], top_ssem.at[7], top_rsem.at[7],
            {"col": 8 * h + n}, (c // 8 == h) if d == 0 else None,
        )
    out_send(0, x1)

    def own_rows(value):
        return jnp.where(h == 0, value[0:4], value[4:8])

    for copy in shared.values():
        copy.wait_send()
    for place in range(6):
        out_sent(place)
    await_bytes(r_last.at[pl.ds(0, 7)], top_ssem.at[7])

    @pl.when(h != c // 8)
    def _():
        await_bytes(r_last.at[7], top_ssem.at[7])

    await_bytes(r_out, out_rsem.at[0])
    for place in range(6):
        for k in range(4):
            value = own_rows(r_out[place, k // 2, k % 2])
            if place == 5:
                out[6, k] = value
            elif place == 4:
                out[5, k] = value
            else:
                out[place + 1, k] = value
    await_bytes(r_last, top_rsem.at[7])
    for q in range(2):
        last = r_last[0, q].astype(F32)
        for zz in range(1, 8):
            last = last + r_last[zz, q].astype(F32)
        for i in range(2):
            out[0, 2 * q + i] = own_rows(last[8 * i : 8 * i + 8])


def on_device(
    right_side, top_right_side, leaf_upper, leaf_upper_mask, leaf_lower, leaf_lower_mask, cross_upper, cross_upper_mask,
    cross_lower, cross_lower_mask, top_upper, top_lower, leaf_upper_inverse, leaf_lower_inverse, top_upper_inverse,
    top_lower_inverse, leaf_sizes, top_sizes,
):
    in_hbm = pl.BlockSpec(memory_space=pl.ANY)
    in_smem = pl.BlockSpec(memory_space=pltpu.SMEM)
    in_vmem = pl.BlockSpec(memory_space=pltpu.VMEM)
    dma = pltpu.SemaphoreType.DMA
    out = pl.pallas_call(
        kernel,
        out_shape=jax.ShapeDtypeStruct((7, 4, 4, 128), F32),
        in_specs=[in_hbm] * 12 + [in_smem] * 6,
        out_specs=in_vmem,
        scratch_shapes=[
            pltpu.VMEM((42, 2, 4, 128, 128), BF),
            pltpu.VMEM((14, 4, 128, 128), F32),
            pltpu.VMEM((14, 4, 128, 256), BF),
            pltpu.VMEM((5, 4, 32, 128), F32),
            pltpu.VMEM((2, 4, 32, 128), F32),
            pltpu.VMEM((7, 32, 512), F32),
            pltpu.VMEM((5, 32, 256), F32),
            pltpu.VMEM((32, 256), F32),
            pltpu.VMEM((5, 4, 128, 128), BF),
            pltpu.VMEM((5, 4, 128, 128), BF),
            pltpu.VMEM((5, 4, 2, 128, 128), BF),
            pltpu.VMEM((4, 4, 32, 128), BF),
            pltpu.VMEM((4, 8, 4, 32, 128), BF),
            pltpu.VMEM((4, 2, 32, 128), BF),
            pltpu.VMEM((4, 4, 2, 32, 128), BF),
            pltpu.VMEM((4, 2, 2, 32, 128), BF),
            pltpu.VMEM((4, 8, 2, 32, 128), BF),
            pltpu.VMEM((5, 2, 32, 128), BF),
            pltpu.VMEM((2, 4, 2, 16, 128), F32),
            pltpu.VMEM((2, 4, 2, 16, 128), F32),
            pltpu.VMEM((2, 16, 128), BF),
            pltpu.VMEM((8, 16, 128), BF),
            pltpu.VMEM((2, 16, 128), BF),
            pltpu.VMEM((8, 2, 16, 128), BF),
            pltpu.VMEM((16, 16, 128), F32),
            pltpu.VMEM((4, 16, 128), F32),
            pltpu.VMEM((4, 2, 16, 128), BF),
            pltpu.VMEM((8, 2, 16, 128), BF),
            pltpu.VMEM((6, 4, 2, 8, 128), F32),
            pltpu.VMEM((6, 2, 2, 8, 128), F32),
        ]
        + [dma((n,)) for n in (20, 8, 8, 4, 4, 4, 4, 4, 4, 5, 5, 5, 5, 5, 5, 5, 5, 8, 8, 6, 1)],
        compiler_params=pltpu.CompilerParams(
            collective_id=0, has_side_effects=True, vmem_limit_bytes=58 * 1024 * 1024
        ),
    )(
        right_side, top_right_side, leaf_upper, leaf_lower, cross_upper, cross_lower, top_upper, top_lower,
        leaf_upper_inverse, leaf_lower_inverse, top_upper_inverse, top_lower_inverse,
        leaf_upper_mask[0, :, 0].T, leaf_lower_mask[0, :, 0].T,
        cross_upper_mask[0, :, 0].transpose(1, 2, 0), cross_lower_mask[0, :, 0].transpose(0, 2, 1),
        leaf_sizes[0].T, top_sizes,
    )
    return out[None, :5], out[5:]


def solution(mesh):
    in_specs = (
        P("rep", None, "row", None, None),
        P(None, "row", None, None),
        P("rep", None, "col", "row", None, None),
        P("rep", None, "col", "row"),
        P("rep", None, "col", "row", None, None),
        P("rep", None, "col", "row"),
        P("rep", None, "col", None, "row", None, None),
        P("rep", None, "col", None, "row"),
        P("rep", None, "col", None, "row", None, None),
        P("rep", None, "col", None, "row"),
        P(None, "col", "row", None, None),
        P(None, "col", "row", None, None),
        P("rep", None, "row", None, None),
        P("rep", None, "row", None, None),
        P(None, "row", None, None),
        P(None, "row", None, None),
        P("rep", None, "row"),
        P(None, "row"),
    )
    out_specs = (P("rep", None, "row", "col", None), P(None, "row", "col", None))
    return jax.shard_map(
        on_device, mesh=mesh, in_specs=in_specs, out_specs=out_specs, check_vma=False
    )
```
